256 devices in a mesh: group: 4 (over y_lo, core), ctx: 64 (over x, z, y_hi).
Axes of the slice: x: 4, y: 4 (y_hi: 2, y_lo: 2; y = y_hi * 2 + y_lo), z: 8, core: 2. Of those that a mesh axis runs over, the one named last changes fastest.
Arguments:
- hidden: bfloat16 [4, 8192, 5120], P('group', 'ctx'), may hold values from -6 to 6
- queries: bfloat16 [4, 8192, 2560], P('group', 'ctx'), may hold values from -300 to 300
- key_value_weight: bfloat16 [5120, 1024], P(('group', 'ctx')), may hold values from -0.078125 to 0.078125
- pooled_hidden_states: bfloat16 [64, 16, 5120], P('ctx'), may hold values from -6 to 6
- group_page_table: int32 [4, 32], P('group'), may hold values from 0 to 63, as said below
- resp_lengths: int32 [4, 8], P('group'), may hold values from 1 to 2048, 8192 in all within a row
Outputs:
- attended: bfloat16 [4, 8192, 2560], P('group', 'ctx')
The draws below stay inside these ranges and needn't reach their ends.
Inputs may be any that keep to these rules, and one draw needn't show every extreme that they name: `group_page_table`: each row names 32 different pages of the pool. `resp_lengths`: each row sums to 8192.
All inputs are finite; a program needn't handle non-finite values.
Results may differ from the reference program's by a relative error of at most 0.012.
The reference program's roundings to bfloat16 on the way count: a program that leaves them out, or rounds other values in their place, can miss the bound.
Values may be sent and summed in bfloat16 or wider, within the bound.
A program may use at most 128 MiB of HBM per device.

```python
import math
import jax
import jax.numpy as jnp
import numpy as np
from jax import lax

MODEL_WIDTH = 5120
QUERY_HEADS = 20
KEY_VALUE_HEADS = 4
HEAD_SIZE = 128
NRESP = 8
PAGE_TOKENS = 16
GROUPS = 4
RESP = 8192
MOST = 2048
POOL_PAGES = 64
PP = 32
PROMPT_TOKENS = 512


def draw_queries(key, part):
    key = jax.random.fold_in(key, 11)
    base_key = jax.random.fold_in(key, 0)
    value_rows = jax.random.normal(base_key, (GROUPS, RESP, QUERY_HEADS, HEAD_SIZE), jnp.float32)
    value_rows = jnp.clip(value_rows, -300.0, 300.0)
    return value_rows.reshape(GROUPS, RESP, QUERY_HEADS * HEAD_SIZE).astype(jnp.bfloat16)


def pick_pages(key):
    inner_key, order_key = jax.random.split(key)
    inner = jax.random.permutation(inner_key, POOL_PAGES - 2)[:PP - 2] + 1
    pages = jnp.concatenate([jnp.array([0, POOL_PAGES - 1], jnp.int32), inner.astype(jnp.int32)])
    return jax.random.permutation(order_key, pages).astype(jnp.int32)


def draw_group_page_table(key, part):
    key = jax.random.fold_in(key, 23)
    group_keys = jax.random.split(key, GROUPS)
    return jax.vmap(pick_pages)(group_keys).astype(jnp.int32)


def levels(rng, extent, pieces, least, top_value):
    gain = 1.0
    for dim, blocks in pieces:
        heights = jax.random.uniform(jax.random.fold_in(jax.random.fold_in(rng, 6), dim), (blocks,), jnp.float32, least / len(pieces), top_value / len(pieces))
        gain = gain * jnp.repeat(jnp.exp(heights), extent[dim] // blocks).reshape((-1,) + (1,) * (len(extent) - 1 - dim))
    return gain


def profile(number_of, total, most, skew):
    portions = [(1 << 20) // math.isqrt(standing ** skew) + 1 for standing in range(2, number_of + 1)]
    surplus, counts = total - most - (number_of - 1), [1] * (number_of - 1)
    while surplus > 0:
        candidates = [i for i in range(number_of - 1) if counts[i] < most]
        mass, budget = sum([portions[i] for i in candidates]), surplus
        for i in candidates:
            addition = min(most - counts[i], max(1, budget * portions[i] // mass), surplus)
            counts[i] = counts[i] + addition
            surplus = surplus - addition
    return np.array([most] + counts)


def uneven_parts(rng, number_of, total, most, skew):
    if number_of == 2:
        one = jax.random.randint(rng, (), max(1, total - most), min(most, total - 1) + 1)
        return jnp.stack([one, total - one])
    sizes = jnp.asarray(profile(number_of, total, most, skew), jnp.int32)
    twos = (number_of - 1) // 2
    giver, receiver = sizes[1:1 + 2 * twos:2], sizes[2:2 + 2 * twos:2]
    room = jnp.minimum(giver - 1, most - receiver)
    moved = jax.random.randint(jax.random.fold_in(rng, 1), (twos,), 0, 1 << 20) % (room + 1)
    sizes = sizes.at[1:1 + 2 * twos:2].set(giver - moved).at[2:2 + 2 * twos:2].set(receiver + moved)
    return sizes[jax.random.permutation(jax.random.fold_in(rng, 2), number_of)]


def gaussian(key, extent, scale, limit, pieces=(), held_as=jnp.bfloat16):
    drawn = jax.random.normal(key, extent, jnp.float32) * scale
    if len(pieces) > 0:
        drawn = levels(key, extent, pieces, -0.22, 0.18) * drawn
    return jnp.clip(drawn, min=-limit, max=limit).astype(held_as)


def setup_inputs(seed: int = 0) -> dict:
    key_list = jax.random.split(jax.random.key(seed), 7)
    hidden = gaussian(key_list[0], (GROUPS, RESP, MODEL_WIDTH), 1.0, 6.0, ((0, 4), (1, 64)))
    queries = draw_queries(jax.random.fold_in(key_list[6], 71), 0)
    key_value_weight = gaussian(key_list[2], (MODEL_WIDTH, 2 * KEY_VALUE_HEADS * HEAD_SIZE), MODEL_WIDTH ** -0.5, 0.078125, ((0, 256),))
    pooled_hidden_states = gaussian(key_list[3], (POOL_PAGES, PAGE_TOKENS, MODEL_WIDTH), 1.0, 6.0, ((0, 64),))
    group_page_table = draw_group_page_table(jax.random.fold_in(key_list[6], 71), 0)
    resp_lengths = jax.vmap(lambda own: uneven_parts(own, NRESP, RESP, MOST, 2))(jax.random.split(key_list[5], GROUPS)).reshape((GROUPS, NRESP)).astype(jnp.int32)
    return {"hidden": hidden, "queries": queries, "key_value_weight": key_value_weight, "pooled_hidden_states": pooled_hidden_states, "group_page_table": group_page_table, "resp_lengths": resp_lengths}


def apply_projection(rows, weight):
    return jnp.dot(rows, weight, preferred_element_type=jnp.float32).astype(jnp.bfloat16)

def response_ids(lengths, positions):
    ends = jnp.cumsum(lengths)
    return lax.optimization_barrier(jnp.sum((positions[:, None] >= ends[None, :]).astype(jnp.int32), axis=1))

def attend_group(query_rows, resp_kv, prompt_key_value, lengths):
    rows_per_block = math.gcd(RESP, 512)
    column_extent = min(RESP, MOST + rows_per_block)
    column_width = KEY_VALUE_HEADS * HEAD_SIZE
    head_group_ratio = QUERY_HEADS // KEY_VALUE_HEADS
    scale = 1.0 / math.sqrt(HEAD_SIZE)
    prompt_key_rows = prompt_key_value[:, :column_width].reshape(PROMPT_TOKENS, KEY_VALUE_HEADS, HEAD_SIZE).astype(jnp.float32)
    prompt_value_rows = prompt_key_value[:, column_width:].reshape(PROMPT_TOKENS, KEY_VALUE_HEADS, HEAD_SIZE).astype(jnp.float32)
    positions = jnp.arange(RESP, dtype=jnp.int32)
    ident = response_ids(lengths, positions)

    def one_block(page_index):
        q_first = (page_index * rows_per_block).astype(jnp.int32)
        k_first = jnp.clip(q_first + rows_per_block - column_extent, 0, RESP - column_extent).astype(jnp.int32)
        query_matrix = lax.dynamic_slice_in_dim(query_rows, q_first, rows_per_block, 0)
        query_matrix = query_matrix.reshape(rows_per_block, KEY_VALUE_HEADS, head_group_ratio, HEAD_SIZE).astype(jnp.float32)
        key_value_rows = lax.dynamic_slice_in_dim(resp_kv, k_first, column_extent, 0)
        key_rows = key_value_rows[:, :column_width].reshape(column_extent, KEY_VALUE_HEADS, HEAD_SIZE).astype(jnp.float32)
        value_rows = key_value_rows[:, column_width:].reshape(column_extent, KEY_VALUE_HEADS, HEAD_SIZE).astype(jnp.float32)
        q_pos = q_first + jnp.arange(rows_per_block, dtype=jnp.int32)
        k_pos = k_first + jnp.arange(column_extent, dtype=jnp.int32)
        q_ids = lax.dynamic_slice_in_dim(ident, q_first, rows_per_block, 0)
        k_ids = lax.dynamic_slice_in_dim(ident, k_first, column_extent, 0)
        live = (k_pos[None, :] <= q_pos[:, None]) & (k_ids[None, :] == q_ids[:, None])
        own_scores = jnp.einsum('qgrd,kgd->grqk', query_matrix, key_rows) * scale
        own_scores = jnp.where(live[None, None], own_scores, -jnp.inf)
        far_scores = jnp.einsum('qgrd,kgd->grqk', query_matrix, prompt_key_rows) * scale
        top = jnp.maximum(lax.optimization_barrier(jnp.max(own_scores, axis=3)), lax.optimization_barrier(jnp.max(far_scores, axis=3)))
        own_weights = jnp.exp(own_scores - top[..., None])
        far_weights = jnp.exp(far_scores - top[..., None])
        total = lax.optimization_barrier(jnp.sum(own_weights, axis=3)) + lax.optimization_barrier(jnp.sum(far_weights, axis=3))
        own_round = lax.optimization_barrier(own_weights.astype(jnp.bfloat16)).astype(jnp.float32)
        far_round = lax.optimization_barrier(far_weights.astype(jnp.bfloat16)).astype(jnp.float32)
        accum = jnp.einsum('grqk,kgd->grqd', own_round, value_rows) + jnp.einsum('grqk,kgd->grqd', far_round, prompt_value_rows)
        mixed = accum / total[..., None]
        return jnp.transpose(mixed, (2, 0, 1, 3)).reshape(rows_per_block, QUERY_HEADS * HEAD_SIZE).astype(jnp.bfloat16)
    blocks = lax.map(one_block, jnp.arange(RESP // rows_per_block, dtype=jnp.int32))
    return blocks.reshape(RESP, QUERY_HEADS * HEAD_SIZE)

def reference(hidden, queries, key_value_weight, pooled_hidden_states, group_page_table, resp_lengths):
    pooled_key_value = apply_projection(pooled_hidden_states.reshape(POOL_PAGES * PAGE_TOKENS, MODEL_WIDTH), key_value_weight).reshape(POOL_PAGES, PAGE_TOKENS, 2 * KEY_VALUE_HEADS * HEAD_SIZE)
    outputs = []
    for page_index in range(GROUPS):
        prompt_key_value = jnp.take(pooled_key_value, group_page_table[page_index], axis=0).reshape(PROMPT_TOKENS, 2 * KEY_VALUE_HEADS * HEAD_SIZE)
        resp_kv = apply_projection(hidden[page_index], key_value_weight)
        outputs.append(attend_group(queries[page_index], resp_kv, prompt_key_value, resp_lengths[page_index]))
    return jnp.stack(outputs, axis=0)
```

```python
import math

import jax
import jax.numpy as jnp
from jax import lax
from jax.experimental import pallas as pl
from jax.experimental.pallas import tpu as pltpu
from jax.sharding import PartitionSpec as P

QUERY_HEADS = 20
KEY_VALUE_HEADS = 4
HEAD_SIZE = 128
DEVICE_TOKENS = 128
PAGE_TOKENS = 16
WIDTH = 5120
ROWS = 2 * DEVICE_TOKENS + PAGE_TOKENS
SIZE = {"x": 4, "y": 4, "z": 8}
ORDERS = (("z", "x", "y"), ("y", "z", "x"), ("x", "y", "z"))
STEPS = 8


def place():
    g, c = lax.axis_index("group"), lax.axis_index("ctx")
    y_lo, core = lax.div(g, 2), lax.rem(g, 2)
    y_hi, z, x = lax.rem(c, 2), lax.rem(lax.div(c, 2), 8), lax.div(c, 16)
    return {"x": x, "y": y_hi * 2 + y_lo, "z": z, "core": core}


def device(at):
    return (
        lax.rem(at["y"], 2) * 2 + at["core"],
        (at["x"] * 8 + at["z"]) * 2 + lax.div(at["y"], 2),
    )


def moved(at, axis, by):
    there = dict(at)
    there[axis] = lax.rem(at[axis] + (by + SIZE[axis]), SIZE[axis])
    return there


def other_core(at):
    return {**at, "core": 1 - at["core"]}


def send(src, dst, send_sem, recv_sem, at):
    return pltpu.make_async_remote_copy(
        src_ref=src,
        dst_ref=dst,
        send_sem=send_sem,
        recv_sem=recv_sem,
        device_id=device(at),
        device_id_type=pl.DeviceIdType.MESH,
    )


def greet(neighbours):
    barrier = pltpu.get_barrier_semaphore()
    for at in neighbours:
        pl.semaphore_signal(
            barrier, inc=1, device_id=device(at), device_id_type=pl.DeviceIdType.MESH
        )
    pl.semaphore_wait(barrier, len(neighbours))


def ring_block(buf, me, axis, done, position, half):
    def pick(name):
        if name == axis:
            return position
        return None if name in done else me[name]

    x, y, z = pick("x"), pick("y"), pick("z")
    everything = slice(None)
    y_lo = everything if y is None else lax.rem(y, 2)
    y_hi = everything if y is None else lax.div(y, 2)
    core = everything if half is None else half
    return buf.at[
        y_lo, core, everything if x is None else x, everything if z is None else z, y_hi
    ]


def ring_plan(order):
    plan = []
    for number, axis in enumerate(order):
        for step in range(1, SIZE[axis] // 2 + 1):
            plan.append((axis, order[:number], step))
    return plan


def project_kernel(
    w_ref, hidden_ref, pool_ref, out_ref,
    ga, gb, gc, rem_ref, rows_ref, perm_ref, main_ref, tail_ref, wide_ref,
    ring_send, ring_recv, pair_send, pair_recv, local_sem,
):
    me = place()
    core = me["core"]
    mate = other_core(me)
    y_lo, y_hi = lax.rem(me["y"], 2), lax.div(me["y"], 2)
    greet([mate] + [moved(me, axis, by) for axis in "xyz" for by in (1, -1)])

    def slot(buf, of_core):
        return buf.at[y_lo, of_core, me["x"], me["z"], y_hi]

    rest = w_ref[16:20, :].astype(jnp.float32)
    for half in range(2):
        pieces = []
        for row in range(4):
            for block in range(4):
                first = (block // 2) * 512 + half * 256 + (block % 2) * 128
                pieces.append(rest[row:row + 1, first:first + 128])
        rem_ref[half] = jnp.concatenate(pieces, axis=0).astype(jnp.bfloat16)

    def shard_parts(half):
        return (
            w_ref.at[pl.ds(0, 16), pl.ds(pl.multiple_of(half * 256, 128), 256)],
            w_ref.at[pl.ds(0, 16), pl.ds(pl.multiple_of(512 + half * 256, 128), 256)],
            rem_ref.at[half],
        )

    bufs = (ga, gb, gc)
    own_rows = pl.ds(pl.multiple_of(core * 128, 128), 128)
    to_mate = [
        send(src, slot(buf, core), pair_send.at[n], pair_recv.at[n], mate)
        for n, (src, buf) in enumerate(zip(shard_parts(1 - core), bufs))
    ]
    stay = [
        pltpu.make_async_copy(src, slot(buf, core), local_sem.at[n])
        for n, (src, buf) in enumerate(zip(shard_parts(core), bufs))
    ]
    for copy in to_mate + stay:
        copy.start()
    rows_out = send(hidden_ref, rows_ref.at[own_rows], pair_send.at[3], pair_recv.at[3], mate)
    rows_stay = pltpu.make_async_copy(hidden_ref, rows_ref.at[own_rows], local_sem.at[3])
    pool_stay = pltpu.make_async_copy(pool_ref, rows_ref.at[pl.ds(256, 16)], local_sem.at[4])
    rows_stay.start()
    pool_stay.start()
    for copy in to_mate:
        copy.wait_recv()
    for copy in stay:
        copy.wait()

    plans = [ring_plan(order) for order in ORDERS]

    def ring_copies(part, number):
        axis, done, step = plans[part][number]
        size = SIZE[axis]
        copies = []
        for way, sign in enumerate((1, -1)):
            half = way if step == size // 2 else None
            out_at = lax.rem(me[axis] + (size - sign * (step - 1)), size)
            src = ring_block(bufs[part], me, axis, done, out_at, half)
            copies.append(
                send(
                    src, src, ring_send.at[part, number, way], ring_recv.at[part, number, way],
                    moved(me, axis, sign),
                )
            )
        return copies

    for number in range(STEPS):
        for part in range(3):
            if number > 0:
                for copy in ring_copies(part, number - 1):
                    copy.wait_recv()
            for copy in ring_copies(part, number):
                copy.start()
        if number == 0:
            rows_out.start()

    row = lax.broadcasted_iota(jnp.int32, (640, 640), 0)
    col = lax.broadcasted_iota(jnp.int32, (640, 640), 1)
    tail = col - 512
    source = jnp.where(
        col < 512,
        20 * lax.shift_right_logical(col, 4) + (col & 15),
        20 * lax.shift_right_logical(tail, 2) + 16 + (tail & 3),
    )
    perm_ref[...] = jnp.where(row == source, 1.0, 0.0).astype(jnp.bfloat16)
    rows_stay.wait()
    pool_stay.wait()
    rows_out.wait_recv()

    def reorder(number, carry):
        block = rows_ref[:, pl.ds(pl.multiple_of(number * 640, 128), 640)]
        turned = jnp.dot(block, perm_ref[...], preferred_element_type=jnp.float32)
        turned = turned.astype(jnp.bfloat16)
        main_ref[:, pl.ds(pl.multiple_of(number * 512, 128), 512)] = turned[:, :512]
        tail_ref[:, pl.ds(pl.multiple_of(number * 128, 128), 128)] = turned[:, 512:]
        return carry

    lax.fori_loop(0, 8, reorder, 0)

    for copy in ring_copies(2, STEPS - 1):
        copy.wait_recv()
    wide_ref[...] = gc[...].reshape(4096, 128).astype(jnp.float32)
    rest = [
        wide_ref[pl.ds(block, 1024, stride=4), :].astype(jnp.bfloat16) for block in range(4)
    ]
    for part in range(2):
        for copy in ring_copies(part, STEPS - 1):
            copy.wait_recv()
        both = jnp.concatenate(rest[2 * part:2 * part + 2], axis=1)
        total = jnp.dot(
            main_ref[...], bufs[part][...].reshape(4096, 256), preferred_element_type=jnp.float32
        )
        total = total + jnp.dot(tail_ref[...], both, preferred_element_type=jnp.float32)
        out_ref[:, 256 * part:256 * part + 256] = total.astype(jnp.bfloat16)

    for copy in to_mate:
        copy.wait_send()
    rows_out.wait_send()
    for number in range(STEPS):
        for part in range(3):
            for copy in ring_copies(part, number):
                copy.wait_send()


def project(weight, hidden, pool):
    return pl.pallas_call(
        project_kernel,
        name="project",
        out_shape=jax.ShapeDtypeStruct((ROWS, 512), jnp.bfloat16),
        in_specs=[
            pl.BlockSpec(memory_space=pltpu.VMEM),
            pl.BlockSpec(memory_space=pl.ANY),
            pl.BlockSpec(memory_space=pl.ANY),
        ],
        out_specs=pl.BlockSpec(memory_space=pltpu.VMEM),
        scratch_shapes=[
            pltpu.VMEM((2, 2, 4, 8, 2, 16, 256), jnp.bfloat16),
            pltpu.VMEM((2, 2, 4, 8, 2, 16, 256), jnp.bfloat16),
            pltpu.VMEM((2, 2, 4, 8, 2, 16, 128), jnp.bfloat16),
            pltpu.VMEM((2, 16, 128), jnp.bfloat16),
            pltpu.VMEM((ROWS, WIDTH), jnp.bfloat16),
            pltpu.VMEM((640, 640), jnp.bfloat16),
            pltpu.VMEM((ROWS, 4096), jnp.bfloat16),
            pltpu.VMEM((ROWS, 1024), jnp.bfloat16),
            pltpu.VMEM((4096, 128), jnp.float32),
            pltpu.SemaphoreType.DMA((3, STEPS, 2)),
            pltpu.SemaphoreType.DMA((3, STEPS, 2)),
            pltpu.SemaphoreType.DMA((4,)),
            pltpu.SemaphoreType.DMA((4,)),
            pltpu.SemaphoreType.DMA((5,)),
        ],
        compiler_params=pltpu.CompilerParams(
            collective_id=0, has_side_effects=True, vmem_limit_bytes=56 * 1024 * 1024
        ),
    )(weight, hidden, pool)


def passed_along(block, axis, distance):
    devices = range(lax.axis_size(axis))
    route = [(i - distance, i) for i in devices if i - distance in devices]
    return lax.ppermute(block, axis, route)


def response_ids(lengths, positions):
    ends = jnp.cumsum(lengths)
    return jnp.sum((positions[:, None] >= ends[None, :]).astype(jnp.int32), axis=1)


def absorb(state, query_matrix, key_rows, value_rows, live, scale):
    top, total, accum = state
    scores = (
        jnp.einsum("qgrd,kgd->grqk", query_matrix, key_rows, preferred_element_type=jnp.float32)
        * scale
    )
    scores = jnp.where(live[None, None], scores, -jnp.inf)
    new_top = jnp.maximum(top, jnp.max(scores, axis=3))
    factor = jnp.exp(top - new_top)
    weights = jnp.exp(scores - new_top[..., None])
    total = total * factor + jnp.sum(weights, axis=3)
    accum = accum * factor[..., None] + jnp.einsum(
        "grqk,kgd->grqd",
        weights.astype(jnp.bfloat16),
        value_rows,
        preferred_element_type=jnp.float32,
    )
    return (new_top, total, accum)


def body(hidden, queries, key_value_weight, pooled_hidden_states, group_page_table, resp_lengths):
    column_width = KEY_VALUE_HEADS * HEAD_SIZE
    scale = 1.0 / math.sqrt(HEAD_SIZE)
    half = project(key_value_weight, hidden[0], pooled_hidden_states[0])
    core = lax.rem(lax.axis_index("group"), 2)
    swap = [(i, i ^ 1) for i in range(4)]
    mine = lax.dynamic_slice_in_dim(half, core * 128, 128, 0)
    theirs = lax.dynamic_slice_in_dim(half, (1 - core) * 128, 128, 0)
    mine = jnp.concatenate([mine, half[256:]], axis=0)
    other = lax.ppermute(jnp.concatenate([theirs, half[256:]], axis=0), "group", swap)
    low, high = jnp.where(core == 0, mine, other), jnp.where(core == 0, other, mine)
    both = jnp.concatenate([low[:, :256], high[:, :256], low[:, 256:], high[:, 256:]], axis=1)
    own_kv, pooled_key_value = both[:128], both[128:]
    pool_all = lax.all_gather(pooled_key_value, "ctx", axis=0, tiled=True).reshape(
        -1, PAGE_TOKENS, 2 * column_width
    )
    prompt_key_value = jnp.take(pool_all, group_page_table[0], axis=0).reshape(-1, 2 * column_width)
    lengths = resp_lengths[0]
    query_matrix = queries[0].reshape(
        DEVICE_TOKENS, KEY_VALUE_HEADS, QUERY_HEADS // KEY_VALUE_HEADS, HEAD_SIZE
    )
    first = lax.axis_index("ctx") * DEVICE_TOKENS
    q_pos = first + jnp.arange(DEVICE_TOKENS, dtype=jnp.int32)
    q_ids = response_ids(lengths, q_pos)
    dimension_list = (KEY_VALUE_HEADS, QUERY_HEADS // KEY_VALUE_HEADS, DEVICE_TOKENS)
    state = (
        jnp.full(dimension_list, -jnp.inf, jnp.float32),
        jnp.zeros(dimension_list, jnp.float32),
        jnp.zeros(dimension_list + (HEAD_SIZE,), jnp.float32),
    )
    prompt_token_rows = prompt_key_value.shape[0]
    prompt_live = jnp.ones((DEVICE_TOKENS, prompt_token_rows), dtype=bool)
    state = absorb(
        state,
        query_matrix,
        prompt_key_value[:, :column_width].reshape(prompt_token_rows, KEY_VALUE_HEADS, HEAD_SIZE),
        prompt_key_value[:, column_width:].reshape(prompt_token_rows, KEY_VALUE_HEADS, HEAD_SIZE),
        prompt_live,
        scale,
    )

    def block_step(carry, key_value_rows, k_first):
        count_of_rows = key_value_rows.shape[0]
        k_pos = k_first + jnp.arange(count_of_rows, dtype=jnp.int32)
        k_ids = response_ids(lengths, k_pos)
        live = (
            (k_pos[None, :] <= q_pos[:, None])
            & (k_pos[None, :] >= 0)
            & (k_ids[None, :] == q_ids[:, None])
        )
        key_rows = key_value_rows[:, :column_width].reshape(
            count_of_rows, KEY_VALUE_HEADS, HEAD_SIZE
        )
        value_rows = key_value_rows[:, column_width:].reshape(
            count_of_rows, KEY_VALUE_HEADS, HEAD_SIZE
        )
        return absorb(carry, query_matrix, key_rows, value_rows, live, scale)

    state = block_step(state, own_kv, first)
    reach_steps = lax.axis_size("ctx") // 4

    def near_step(page_index, carry):
        moving, inner_state = carry
        moving = passed_along(moving, "ctx", 1)
        return (moving, block_step(inner_state, moving, first - (page_index + 1) * DEVICE_TOKENS))

    state = lax.fori_loop(0, reach_steps, near_step, (own_kv, state))[1]
    mixed = state[2] / state[1][..., None]
    return (
        jnp.transpose(mixed, (2, 0, 1, 3))
        .reshape(1, DEVICE_TOKENS, QUERY_HEADS * HEAD_SIZE)
        .astype(jnp.bfloat16)
    )


def solution(mesh):
    in_specs = (
        P("group", "ctx", None),
        P("group", "ctx", None),
        P(("group", "ctx"), None),
        P("ctx", None, None),
        P("group", None),
        P("group", None),
    )
    out_specs = P("group", "ctx", None)
    return jax.shard_map(body, mesh=mesh, in_specs=in_specs, out_specs=out_specs, check_vma=False)
```

```python
import math

import jax
import jax.numpy as jnp
from jax import lax
from jax.experimental import pallas as pl
from jax.experimental.pallas import tpu as pltpu
from jax.sharding import PartitionSpec as P

QUERY_HEADS = 20
KEY_VALUE_HEADS = 4
HEAD_SIZE = 128
DEVICE_TOKENS = 128
PAGE_TOKENS = 16
WIDTH = 5120
ROWS = 2 * DEVICE_TOKENS + PAGE_TOKENS
SIZE = {"x": 4, "y": 4, "z": 8}
ORDERS = (("z", "x", "y"), ("y", "z", "x"), ("x", "y", "z"))
STEPS = 8


def place():
    g, c = lax.axis_index("group"), lax.axis_index("ctx")
    y_lo, core = lax.div(g, 2), lax.rem(g, 2)
    y_hi, z, x = lax.rem(c, 2), lax.rem(lax.div(c, 2), 8), lax.div(c, 16)
    return {"x": x, "y": y_hi * 2 + y_lo, "z": z, "core": core}


def device(at):
    return (
        lax.rem(at["y"], 2) * 2 + at["core"],
        (at["x"] * 8 + at["z"]) * 2 + lax.div(at["y"], 2),
    )


def moved(at, axis, by):
    there = dict(at)
    there[axis] = lax.rem(at[axis] + (by + SIZE[axis]), SIZE[axis])
    return there


def other_core(at):
    return {**at, "core": 1 - at["core"]}


def send(src, dst, send_sem, recv_sem, at):
    return pltpu.make_async_remote_copy(
        src_ref=src,
        dst_ref=dst,
        send_sem=send_sem,
        recv_sem=recv_sem,
        device_id=device(at),
        device_id_type=pl.DeviceIdType.MESH,
    )


def greet(neighbours):
    barrier = pltpu.get_barrier_semaphore()
    for at in neighbours:
        pl.semaphore_signal(
            barrier, inc=1, device_id=device(at), device_id_type=pl.DeviceIdType.MESH
        )
    pl.semaphore_wait(barrier, len(neighbours))


def ring_block(buf, me, axis, done, position, half):
    def pick(name):
        if name == axis:
            return position
        return None if name in done else me[name]

    x, y, z = pick("x"), pick("y"), pick("z")
    everything = slice(None)
    y_lo = everything if y is None else lax.rem(y, 2)
    y_hi = everything if y is None else lax.div(y, 2)
    core = everything if half is None else half
    return buf.at[
        y_lo, core, everything if x is None else x, everything if z is None else z, y_hi
    ]


def ring_plan(order):
    plan = []
    for number, axis in enumerate(order):
        for step in range(1, SIZE[axis] // 2 + 1):
            plan.append((axis, order[:number], step))
    return plan


def project_kernel(
    w_ref, hidden_ref, pool_ref, out_ref,
    ga, gb, gc, rem_ref, rows_ref, perm_ref, main_ref, tail_ref, wide_ref,
    ring_send, ring_recv, pair_send, pair_recv, local_sem,
):
    me = place()
    core = me["core"]
    mate = other_core(me)
    y_lo, y_hi = lax.rem(me["y"], 2), lax.div(me["y"], 2)
    greet([mate] + [moved(me, axis, by) for axis in "xyz" for by in (1, -1)])

    def slot(buf, of_core):
        return buf.at[y_lo, of_core, me["x"], me["z"], y_hi]

    rest = w_ref[16:20, :].astype(jnp.float32)
    for half in range(2):
        pieces = []
        for row in range(4):
            for block in range(4):
                first = (block // 2) * 512 + half * 256 + (block % 2) * 128
                pieces.append(rest[row:row + 1, first:first + 128])
        rem_ref[half] = jnp.concatenate(pieces, axis=0).astype(jnp.bfloat16)

    def shard_parts(half):
        return (
            w_ref.at[pl.ds(0, 16), pl.ds(pl.multiple_of(half * 256, 128), 256)],
            w_ref.at[pl.ds(0, 16), pl.ds(pl.multiple_of(512 + half * 256, 128), 256)],
            rem_ref.at[half],
        )

    bufs = (ga, gb, gc)
    own_rows = pl.ds(pl.multiple_of(core * 128, 128), 128)
    to_mate = [
        send(src, slot(buf, core), pair_send.at[n], pair_recv.at[n], mate)
        for n, (src, buf) in enumerate(zip(shard_parts(1 - core), bufs))
    ]
    stay = [
        pltpu.make_async_copy(src, slot(buf, core), local_sem.at[n])
        for n, (src, buf) in enumerate(zip(shard_parts(core), bufs))
    ]
    for copy in to_mate + stay:
        copy.start()
    rows_out = send(hidden_ref, rows_ref.at[own_rows], pair_send.at[3], pair_recv.at[3], mate)
    rows_stay = pltpu.make_async_copy(hidden_ref, rows_ref.at[own_rows], local_sem.at[3])
    pool_stay = pltpu.make_async_copy(pool_ref, rows_ref.at[pl.ds(256, 16)], local_sem.at[4])
    rows_stay.start()
    pool_stay.start()
    for copy in to_mate:
        copy.wait_recv()
    for copy in stay:
        copy.wait()

    plans = [ring_plan(order) for order in ORDERS]

    def ring_copies(part, number):
        axis, done, step = plans[part][number]
        size = SIZE[axis]
        copies = []
        for way, sign in enumerate((1, -1)):
            half = way if step == size // 2 else None
            out_at = lax.rem(me[axis] + (size - sign * (step - 1)), size)
            src = ring_block(bufs[part], me, axis, done, out_at, half)
            copies.append(
                send(
                    src, src, ring_send.at[part, number, way], ring_recv.at[part, number, way],
                    moved(me, axis, sign),
                )
            )
        return copies

    for number in range(STEPS):
        for part in range(3):
            if number > 0:
                for copy in ring_copies(part, number - 1):
                    copy.wait_recv()
            for copy in ring_copies(part, number):
                copy.start()
        if number == 0:
            rows_out.start()

    row = lax.broadcasted_iota(jnp.int32, (640, 640), 0)
    col = lax.broadcasted_iota(jnp.int32, (640, 640), 1)
    tail = col - 512
    source = jnp.where(
        col < 512,
        20 * lax.shift_right_logical(col, 4) + (col & 15),
        20 * lax.shift_right_logical(tail, 2) + 16 + (tail & 3),
    )
    perm_ref[...] = jnp.where(row == source, 1.0, 0.0).astype(jnp.bfloat16)
    rows_stay.wait()
    pool_stay.wait()
    rows_out.wait_recv()

    def reorder(number, carry):
        block = rows_ref[:, pl.ds(pl.multiple_of(number * 640, 128), 640)]
        turned = jnp.dot(block, perm_ref[...], preferred_element_type=jnp.float32)
        turned = turned.astype(jnp.bfloat16)
        main_ref[:, pl.ds(pl.multiple_of(number * 512, 128), 512)] = turned[:, :512]
        tail_ref[:, pl.ds(pl.multiple_of(number * 128, 128), 128)] = turned[:, 512:]
        return carry

    lax.fori_loop(0, 8, reorder, 0)

    for copy in ring_copies(2, STEPS - 1):
        copy.wait_recv()
    wide_ref[...] = gc[...].reshape(4096, 128).astype(jnp.float32)
    rest = [
        wide_ref[pl.ds(block, 1024, stride=4), :].astype(jnp.bfloat16) for block in range(4)
    ]
    for part in range(2):
        for copy in ring_copies(part, STEPS - 1):
            copy.wait_recv()
        both = jnp.concatenate(rest[2 * part:2 * part + 2], axis=1)
        total = jnp.dot(
            main_ref[...], bufs[part][...].reshape(4096, 256), preferred_element_type=jnp.float32
        )
        total = total + jnp.dot(tail_ref[...], both, preferred_element_type=jnp.float32)
        out_ref[:, 256 * part:256 * part + 256] = total.astype(jnp.bfloat16)

    for copy in to_mate:
        copy.wait_send()
    rows_out.wait_send()
    for number in range(STEPS):
        for part in range(3):
            for copy in ring_copies(part, number):
                copy.wait_send()


def project(weight, hidden, pool):
    return pl.pallas_call(
        project_kernel,
        name="project",
        out_shape=jax.ShapeDtypeStruct((ROWS, 512), jnp.bfloat16),
        in_specs=[
            pl.BlockSpec(memory_space=pltpu.VMEM),
            pl.BlockSpec(memory_space=pl.ANY),
            pl.BlockSpec(memory_space=pl.ANY),
        ],
        out_specs=pl.BlockSpec(memory_space=pltpu.VMEM),
        scratch_shapes=[
            pltpu.VMEM((2, 2, 4, 8, 2, 16, 256), jnp.bfloat16),
            pltpu.VMEM((2, 2, 4, 8, 2, 16, 256), jnp.bfloat16),
            pltpu.VMEM((2, 2, 4, 8, 2, 16, 128), jnp.bfloat16),
            pltpu.VMEM((2, 16, 128), jnp.bfloat16),
            pltpu.VMEM((ROWS, WIDTH), jnp.bfloat16),
            pltpu.VMEM((640, 640), jnp.bfloat16),
            pltpu.VMEM((ROWS, 4096), jnp.bfloat16),
            pltpu.VMEM((ROWS, 1024), jnp.bfloat16),
            pltpu.VMEM((4096, 128), jnp.float32),
            pltpu.SemaphoreType.DMA((3, STEPS, 2)),
            pltpu.SemaphoreType.DMA((3, STEPS, 2)),
            pltpu.SemaphoreType.DMA((4,)),
            pltpu.SemaphoreType.DMA((4,)),
            pltpu.SemaphoreType.DMA((5,)),
        ],
        compiler_params=pltpu.CompilerParams(
            collective_id=0, has_side_effects=True, vmem_limit_bytes=56 * 1024 * 1024
        ),
    )(weight, hidden, pool)


SCALE = math.log2(math.e) / math.sqrt(HEAD_SIZE)
HALF_HEADS = QUERY_HEADS // 2
HALF_WIDTH = HALF_HEADS * HEAD_SIZE
PAIR = 2 * DEVICE_TOKENS


def along(me, by):
    at = lax.rem(me["x"] * 8 + me["z"] + (32 + by), 32)
    return {**me, "x": lax.div(at, 8), "z": lax.rem(at, 8)}


def slot_of(back):
    return 0 if back == 0 else 2 * back - 1 if back <= 4 else 2 * (9 - back)


def attend_kernel(
    half_ref, queries_ref, pages_ref, lengths_ref, out_ref,
    kv_ref, pool_ref, query_ref, give_ref, bias_ref, top_ref, total_ref, sum_ref,
    group_send, group_recv, query_send, query_recv, local_sem,
    halo_send, halo_recv, pool_send, pool_recv, give_send, give_recv,
):
    me = place()
    core = me["core"]
    y_lo, y_hi = lax.rem(me["y"], 2), lax.div(me["y"], 2)
    pair = me["x"] * 8 + me["z"]
    partner = {**me, "y": (1 - y_hi) * 2 + y_lo}
    greet(
        [other_core(me), partner, other_core(partner), along(me, 1), along(me, -1)]
        + [moved(me, axis, by) for axis in "xz" for by in (1, -1)]
    )

    def half_columns(ref, of):
        return ref.at[:, pl.ds(pl.multiple_of(of * HALF_WIDTH, 128), HALF_WIDTH)]

    query_out = send(
        half_columns(queries_ref, 1 - y_hi), query_ref.at[y_hi], query_send, query_recv, partner
    )
    query_stay = pltpu.make_async_copy(
        half_columns(queries_ref, y_hi), query_ref.at[y_hi], local_sem
    )

    def regroup(to_core, what, from_hi):
        if what == 0:
            src = half_ref.at[pl.ds(to_core * 128, 128)]
            dst = kv_ref.at[0, pl.ds(pl.multiple_of(from_hi * 128, 128), 128)]
        else:
            src = half_ref.at[pl.ds(256, 16)]
            dst = pool_ref.at[pair * 2 + from_hi]
        return send(
            src, dst, group_send.at[to_core, what], group_recv.at[from_hi, what],
            {**me, "y": core * 2 + y_lo, "core": jnp.int32(to_core)},
        )

    for what in (1, 0):
        for to_core in range(2):
            stays = jnp.logical_and(core == y_hi, core == to_core)

            @pl.when(stays)
            def _():
                copy = regroup(to_core, what, y_hi)
                pltpu.make_async_copy(copy.src_ref, copy.dst_ref, group_recv.at[y_hi, what]).start()

            @pl.when(jnp.logical_not(stays))
            def _():
                regroup(to_core, what, y_hi).start()

    query_out.start()
    query_stay.start()

    pool_plan = ring_plan(("z", "x"))

    def pool_copies(number):
        axis, _, step = pool_plan[number]
        size = SIZE[axis]
        copies = []
        for way, sign in enumerate((1, -1)):
            at = lax.rem(me[axis] + (size - sign * (step - 1)), size)
            count = 2 if axis == "z" else 16
            first = (me["x"] * 8 + at) * 2 if axis == "z" else at * 16
            if step == size // 2:
                count = count // 2
                first = first + way * count
            block = pool_ref.at[pl.ds(first, count)]
            copies.append(
                send(
                    block, block, pool_send.at[number, way], pool_recv.at[number, way],
                    moved(me, axis, sign),
                )
            )
        return copies

    def pool_step(number):
        if number > 0:
            for copy in pool_copies(number - 1):
                copy.wait_recv()
        if number < len(pool_plan):
            for copy in pool_copies(number):
                copy.start()

    def forth(step):
        return send(
            kv_ref.at[slot_of(step - 1)], kv_ref.at[slot_of(step)],
            halo_send.at[step - 1], halo_recv.at[step - 1], along(me, 1),
        )

    def back(step):
        if step == 0:
            src, to = kv_ref.at[slot_of(0)], moved_pair
        else:
            src, to = kv_ref.at[slot_of(9 - step)], along(me, -1)
        return send(
            src, kv_ref.at[slot_of(8 - step)], halo_send.at[4 + step], halo_recv.at[4 + step], to
        )

    moved_pair = moved(me, "x", 1)

    for what in (1, 0):
        for from_hi in range(2):
            regroup(0, what, jnp.int32(from_hi)).wait_recv()
        if what == 1:
            pool_step(0)
    forth(1).start()
    back(0).start()

    row = lax.broadcasted_iota(jnp.int32, (PAIR, PAIR), 0)
    lane = lax.broadcasted_iota(jnp.int32, (PAIR, PAIR), 1)
    position = pair * PAIR + row
    begin = jnp.zeros((PAIR, PAIR), jnp.int32)
    end = jnp.int32(0)
    for number in range(8):
        end = end + lengths_ref[0, number]
        begin = jnp.where(position >= end, end, begin)

    def bias_of(back_by):
        key = (pair - back_by) * PAIR + lane
        live = key >= begin
        if back_by == 0:
            live = jnp.logical_and(live, key <= position)
        return jnp.where(live, 0.0, -jnp.inf).astype(jnp.float32)

    top_ref[...] = jnp.full(top_ref.shape, -jnp.inf, jnp.float32)
    total_ref[...] = jnp.zeros(total_ref.shape, jnp.float32)
    sum_ref[...] = jnp.zeros(sum_ref.shape, jnp.float32)

    def attend(first, count, masked, head):
        rows = count * PAIR

        def one(number, carry):
            column = pl.multiple_of((head * 5 + number) * 128, 128)
            at = head * 5 + number
            query = query_ref[:, :, pl.ds(column, 128)].reshape(PAIR, 128)
            key = kv_ref[first:first + count, :, head * 128:head * 128 + 128].reshape(rows, 128)
            value = kv_ref[first:first + count, :, 256 + head * 128:384 + head * 128]
            score = lax.dot_general(
                query, key, (((1,), (1,)), ((), ())), preferred_element_type=jnp.float32
            )
            if masked:
                score = score + bias_ref[:, :rows]
            old = top_ref[at]
            new = jnp.maximum(old, jnp.max(score, axis=1, keepdims=True))
            factor = jnp.exp2((old - new) * SCALE)
            weight = jnp.exp2((score - jnp.concatenate([new] * (rows // 128), axis=1)) * SCALE)
            part = weight[:, :128]
            for lanes in range(128, rows, 128):
                part = part + weight[:, lanes:lanes + 128]
            top_ref[at] = new
            total_ref[at] = total_ref[at] * factor + part
            sum_ref[at] = sum_ref[at] * factor + jnp.dot(
                weight.astype(jnp.bfloat16), value.reshape(rows, 128),
                preferred_element_type=jnp.float32,
            )
            return carry

        lax.fori_loop(0, 5, one, 0, unroll=5)

    def finish(head):
        for number in range(5):
            at = head * 5 + number
            total = jnp.sum(total_ref[at], axis=1, keepdims=True)
            done = (sum_ref[at] / total).astype(jnp.bfloat16).reshape(2, 128, 128)
            for hi in range(2):
                @pl.when(y_hi == hi)
                def _():
                    first = hi * HALF_WIDTH + at * 128
                    out_ref[:, first:first + 128] = done[hi]
                    give_ref[:, at * 128:at * 128 + 128] = done[1 - hi]

    def give(head):
        first = pl.multiple_of(y_hi * HALF_WIDTH + head * 640, 128)
        return send(
            give_ref.at[:, pl.ds(head * 640, 640)], out_ref.at[:, pl.ds(first, 640)],
            give_send.at[head], give_recv.at[head], partner,
        )

    pool_step(1)
    query_out.wait_recv()
    query_stay.wait()
    bias_ref[:, :PAIR] = bias_of(0)
    for head in range(2):
        attend(0, 1, True, head)
        if head == 0:
            pool_step(2)
    for step in range(1, 5):
        forth(step).wait_recv()
        back(step - 1).wait_recv()
        if step < 4:
            forth(step + 1).start()
            back(step).start()
        if step < 4:
            pool_step(step * 2 + 1 if step < 3 else 6)
        bias_ref[:, :PAIR] = bias_of(step)
        bias_ref[:, PAIR:] = bias_of(9 - step)
        for head in range(2):
            attend(2 * step - 1, 2, True, head)
            if head == 0 and step < 2:
                pool_step(step * 2 + 2)
            if step == 4:
                finish(head)
                give(head).start()
        if step == 3:
            def page(number, carry):
                first = pl.multiple_of(lax.rem(number, 16) * 16, 16)
                kv_ref[9 + lax.div(number, 16), pl.ds(first, 16)] = pool_ref[pages_ref[0, number]]
                return carry

            lax.fori_loop(0, 32, page, 0)
            for head in range(2):
                attend(9, 2, False, head)

    for head in range(2):
        give(head).wait()
    query_out.wait_send()
    for what in range(2):
        for to_core in range(2):
            @pl.when(jnp.logical_not(jnp.logical_and(core == y_hi, core == to_core)))
            def _():
                regroup(to_core, what, y_hi).wait_send()
    for number in range(len(pool_plan)):
        for copy in pool_copies(number):
            copy.wait_send()
    for step in range(1, 5):
        forth(step).wait_send()
        back(step - 1).wait_send()


def attend_all(half, queries, pages, lengths):
    return pl.pallas_call(
        attend_kernel,
        name="attend",
        out_shape=jax.ShapeDtypeStruct((DEVICE_TOKENS, QUERY_HEADS * HEAD_SIZE), jnp.bfloat16),
        in_specs=[
            pl.BlockSpec(memory_space=pltpu.VMEM),
            pl.BlockSpec(memory_space=pl.ANY),
            pl.BlockSpec(memory_space=pltpu.SMEM),
            pl.BlockSpec(memory_space=pltpu.SMEM),
        ],
        out_specs=pl.BlockSpec(memory_space=pltpu.VMEM),
        scratch_shapes=[
            pltpu.VMEM((11, PAIR, 512), jnp.bfloat16),
            pltpu.VMEM((64, PAGE_TOKENS, 512), jnp.bfloat16),
            pltpu.VMEM((2, DEVICE_TOKENS, HALF_WIDTH), jnp.bfloat16),
            pltpu.VMEM((DEVICE_TOKENS, HALF_WIDTH), jnp.bfloat16),
            pltpu.VMEM((PAIR, 2 * PAIR), jnp.float32),
            pltpu.VMEM((HALF_HEADS, PAIR, 128), jnp.float32),
            pltpu.VMEM((HALF_HEADS, PAIR, 128), jnp.float32),
            pltpu.VMEM((HALF_HEADS, PAIR, 128), jnp.float32),
            pltpu.SemaphoreType.DMA((2, 2)),
            pltpu.SemaphoreType.DMA((2, 2)),
            pltpu.SemaphoreType.DMA,
            pltpu.SemaphoreType.DMA,
            pltpu.SemaphoreType.DMA,
            pltpu.SemaphoreType.DMA((8,)),
            pltpu.SemaphoreType.DMA((8,)),
            pltpu.SemaphoreType.DMA((6, 2)),
            pltpu.SemaphoreType.DMA((6, 2)),
            pltpu.SemaphoreType.DMA((2,)),
            pltpu.SemaphoreType.DMA((2,)),
        ],
        compiler_params=pltpu.CompilerParams(
            collective_id=1, has_side_effects=True, vmem_limit_bytes=48 * 1024 * 1024
        ),
    )(half, queries, pages, lengths)


def body(hidden, queries, key_value_weight, pooled_hidden_states, group_page_table, resp_lengths):
    half = project(key_value_weight, hidden[0], pooled_hidden_states[0])
    return attend_all(half, queries[0], group_page_table, resp_lengths)[None]


def solution(mesh):
    in_specs = (
        P("group", "ctx", None),
        P("group", "ctx", None),
        P(("group", "ctx"), None),
        P("ctx", None, None),
        P("group", None),
        P("group", None),
    )
    out_specs = P("group", "ctx", None)
    return jax.shard_map(body, mesh=mesh, in_specs=in_specs, out_specs=out_specs, check_vma=False)
```

```python
import math

import jax
import jax.numpy as jnp
from jax import lax
from jax.experimental import pallas as pl
from jax.experimental.pallas import tpu as pltpu
from jax.sharding import PartitionSpec as P

QUERY_HEADS = 20
KEY_VALUE_HEADS = 4
HEAD_SIZE = 128
DEVICE_TOKENS = 128
PAGE_TOKENS = 16
WIDTH = 5120
SCALE = math.log2(math.e) / math.sqrt(HEAD_SIZE)
HALF_HEADS = QUERY_HEADS // 2
HALF_WIDTH = HALF_HEADS * HEAD_SIZE
PAIR = 2 * DEVICE_TOKENS
CHUNKS = 4
CHUNK = PAIR // CHUNKS
ROWS = 2 * DEVICE_TOKENS + PAGE_TOKENS
SIZE = {"x": 4, "y": 4, "z": 8}
ORDERS = (("z", "x", "y"), ("z", "x", "y"), ("z", "y", "x"), ("z", "y", "x"), ("x", "y", "z"))
PARTS = len(ORDERS)


def place():
    g, c = lax.axis_index("group"), lax.axis_index("ctx")
    y_lo, core = lax.div(g, 2), lax.rem(g, 2)
    y_hi, z, x = lax.rem(c, 2), lax.rem(lax.div(c, 2), 8), lax.div(c, 16)
    return {"x": x, "y": y_hi * 2 + y_lo, "z": z, "core": core}


def device(at):
    return (
        lax.rem(at["y"], 2) * 2 + at["core"],
        (at["x"] * 8 + at["z"]) * 2 + lax.div(at["y"], 2),
    )


def moved(at, axis, by):
    there = dict(at)
    there[axis] = lax.rem(at[axis] + (by + SIZE[axis]), SIZE[axis])
    return there


def other_core(at):
    return {**at, "core": 1 - at["core"]}


def send(src, dst, send_sem, recv_sem, at):
    return pltpu.make_async_remote_copy(
        src_ref=src,
        dst_ref=dst,
        send_sem=send_sem,
        recv_sem=recv_sem,
        device_id=device(at),
        device_id_type=pl.DeviceIdType.MESH,
    )


def ring_block(buf, me, axis, done, position, half):
    def pick(name):
        if name == axis:
            return position
        return None if name in done else me[name]

    x, y, z = pick("x"), pick("y"), pick("z")
    everything = slice(None)
    y_lo = everything if y is None else lax.rem(y, 2)
    y_hi = everything if y is None else lax.div(y, 2)
    core = everything if half is None else half
    return buf.at[
        y_lo, core, everything if x is None else x, everything if z is None else z, y_hi
    ]


def along(me, by):
    at = lax.rem(me["x"] * 8 + me["z"] + (32 + by), 32)
    return {**me, "x": lax.div(at, 8), "z": lax.rem(at, 8)}


def slot_of(back):
    return 0 if back == 0 else 2 * back - 1 if back <= 4 else 2 * (9 - back)


def kernel(
    w_ref, hidden_ref, pages_in_ref, queries_ref, table_ref, lengths_ref, out_ref,
    ga, gb, gc, gd, ge, rem_ref, rows_ref, perm_ref, main_ref, tail_ref, wide_ref, half_ref,
    kv_ref, pool_ref, query_ref, give_ref, bias_ref, begin_ref, top_ref, total_ref, sum_ref,
    weight_send, weight_recv, mate_send, mate_recv, local_sem,
    group_send, group_recv, query_send, query_recv,
    halo_send, halo_recv, pool_send, pool_recv, give_send, give_recv,
):
    me = place()
    core = me["core"]
    mate = other_core(me)
    y_lo, y_hi = lax.rem(me["y"], 2), lax.div(me["y"], 2)
    pair = me["x"] * 8 + me["z"]
    partner = moved(me, "y", 2)
    neighbours = [mate, other_core(partner), along(me, 1), along(me, -1)] + [
        moved(me, axis, by) for axis in "xyz" for by in range(1, SIZE[axis])
    ]
    barrier = pltpu.get_barrier_semaphore()
    for at in neighbours:
        pl.semaphore_signal(
            barrier, inc=1, device_id=device(at), device_id_type=pl.DeviceIdType.MESH
        )

    own_rows = pl.ds(pl.multiple_of(core * 128, 128), 128)
    rows_stay = pltpu.make_async_copy(hidden_ref, rows_ref.at[own_rows], local_sem.at[5])
    pool_stay = pltpu.make_async_copy(pages_in_ref, rows_ref.at[pl.ds(256, 16)], local_sem.at[6])
    rows_stay.start()
    pool_stay.start()
    rest = w_ref[16:20, :].astype(jnp.float32)
    for half in range(2):
        pieces = []
        for row in range(4):
            for block in range(4):
                first = (block // 2) * 512 + half * 256 + (block % 2) * 128
                pieces.append(rest[row:row + 1, first:first + 128])
        rem_ref[half] = jnp.concatenate(pieces, axis=0).astype(jnp.bfloat16)
    row = lax.broadcasted_iota(jnp.int32, (640, 640), 0)
    col = lax.broadcasted_iota(jnp.int32, (640, 640), 1)
    last = col - 512
    source = jnp.where(
        col < 512,
        20 * lax.shift_right_logical(col, 4) + (col & 15),
        20 * lax.shift_right_logical(last, 2) + 16 + (last & 3),
    )
    perm_ref[...] = jnp.where(row == source, 1.0, 0.0).astype(jnp.bfloat16)
    pl.semaphore_wait(barrier, len(neighbours))

    bufs = (ga, gb, gc, gd, ge)

    def slot(buf, of_core):
        return buf.at[y_lo, of_core, me["x"], me["z"], y_hi]

    def shard_parts(half):
        starts = (half * 256, half * 256 + 128, half * 256 + 512, half * 256 + 640)
        return [
            w_ref.at[pl.ds(0, 16), pl.ds(pl.multiple_of(start, 128), 128)] for start in starts
        ] + [rem_ref.at[half]]

    to_mate = [
        send(src, slot(buf, core), mate_send.at[n], mate_recv.at[n], mate)
        for n, (src, buf) in enumerate(zip(shard_parts(1 - core), bufs))
    ]
    stay = [
        pltpu.make_async_copy(src, slot(buf, core), local_sem.at[n])
        for n, (src, buf) in enumerate(zip(shard_parts(core), bufs))
    ]
    for copy in to_mate + stay:
        copy.start()

    def direct(part, phase):
        order = ORDERS[part]
        axis, done = order[phase], order[:phase]
        base = 0 if phase == 0 else SIZE[order[0]] - 1
        block = ring_block(bufs[part], me, axis, done, me[axis], None)
        return [
            send(
                block, block, weight_send.at[part, base + by - 1],
                weight_recv.at[part, base + by - 1], moved(me, axis, by),
            )
            for by in range(1, SIZE[axis])
        ]

    def ring(part, step, way, half):
        order = ORDERS[part]
        axis, size = order[2], SIZE[order[2]]
        sign = 1 - 2 * way
        index = SIZE[order[0]] + SIZE[order[1]] - 2 + ((step - 1) * 2 + way) * 2 + half
        at = lax.rem(me[axis] + (size - sign * (step - 1)), size)
        block = ring_block(bufs[part], me, axis, order[:2], at, half)
        return send(
            block, block, weight_send.at[part, index], weight_recv.at[part, index],
            moved(me, axis, sign),
        )

    def ring_steps(part):
        return SIZE[ORDERS[part][2]] // 2

    def ring_sends(part):
        steps = ring_steps(part)
        return [
            (step, way, half)
            for step in range(1, steps + 1) for way in range(2) for half in range(2)
            if step < steps or half == way
        ]

    def second(part):
        for copy in direct(part, 0):
            copy.wait_recv()
        for copy in direct(part, 1):
            copy.start()

    def third(part):
        for copy in direct(part, 1):
            copy.wait_recv()
        for turn in range(2):
            for way in range(2):
                ring(part, 1, way, way ^ turn).start()

    def pass_on(part, step, turn):
        for way in range(2):
            ring(part, step, way, way ^ turn).wait_recv()
            if step + 1 < ring_steps(part) or turn == 0:
                ring(part, step + 1, way, way ^ turn).start()

    def close(part):
        steps = ring_steps(part)
        for way in range(2):
            ring(part, steps - 1, way, 1 - way).wait_recv()
        for way in range(2):
            ring(part, steps, way, way).wait_recv()

    for part in (4, 0, 2, 1, 3):
        to_mate[part].wait_recv()
        stay[part].wait()
        for copy in direct(part, 0):
            copy.start()
    rows_out = send(hidden_ref, rows_ref.at[own_rows], mate_send.at[5], mate_recv.at[5], mate)
    rows_out.start()

    def half_columns(ref, of):
        return ref.at[:, pl.ds(pl.multiple_of(of * HALF_WIDTH, 128), HALF_WIDTH)]

    query_out = send(
        half_columns(queries_ref, 1 - y_hi), query_ref.at[y_hi], query_send, query_recv, partner
    )
    query_stay = pltpu.make_async_copy(
        half_columns(queries_ref, y_hi), query_ref.at[y_hi], local_sem.at[7]
    )
    query_stay.start()

    def reorder(first, count):
        def one(number, carry):
            block = rows_ref[:, pl.ds(pl.multiple_of(number * 640, 128), 640)]
            turned = jnp.dot(block, perm_ref[...], preferred_element_type=jnp.float32)
            turned = turned.astype(jnp.bfloat16)
            main_ref[:, pl.ds(pl.multiple_of(number * 512, 128), 512)] = turned[:, :512]
            tail_ref[:, pl.ds(pl.multiple_of(number * 128, 128), 128)] = turned[:, 512:]
            return carry

        lax.fori_loop(first, first + count, one, 0)

    second(4)
    second(0)
    second(2)
    rows_stay.wait()
    pool_stay.wait()
    third(4)
    second(1)
    second(3)
    pass_on(4, 1, 0)
    pass_on(4, 1, 1)
    third(0)
    third(2)
    rows_out.wait_recv()
    reorder(0, 2)
    pass_on(4, 2, 0)
    third(1)
    third(3)
    pass_on(4, 2, 1)
    reorder(2, 2)
    pass_on(0, 1, 0)
    pass_on(2, 1, 0)
    pass_on(4, 3, 0)
    reorder(4, 2)
    pass_on(1, 1, 0)
    pass_on(3, 1, 0)
    reorder(6, 2)

    token = lax.broadcasted_iota(jnp.int32, (PAIR, PAIR), 0)
    lane = lax.broadcasted_iota(jnp.int32, (PAIR, PAIR), 1)
    position = pair * PAIR + token
    begin = jnp.zeros((PAIR, PAIR), jnp.int32)
    end = jnp.int32(0)
    for number in range(8):
        end = end + lengths_ref[0, number]
        begin = jnp.where(position >= end, end, begin)
    begin_ref[...] = begin
    top_ref[...] = jnp.full(top_ref.shape, -jnp.inf, jnp.float32)
    total_ref[...] = jnp.zeros(total_ref.shape, jnp.float32)
    sum_ref[...] = jnp.zeros(sum_ref.shape, jnp.float32)

    def bias_of(back_by):
        key = (pair - back_by) * PAIR + lane
        live = key >= begin_ref[...]
        if back_by == 0:
            live = jnp.logical_and(live, key <= position)
        return jnp.where(live, 0.0, -jnp.inf).astype(jnp.float32)

    bias_ref[:, :PAIR] = bias_of(0)

    close(4)
    wide_ref[...] = ge[...].reshape(4096, 128).astype(jnp.float32)
    rest = [
        wide_ref[pl.ds(block, 1024, stride=4), :].astype(jnp.bfloat16) for block in range(4)
    ]
    for first in (0, 2):
        both = []
        for part in (first, first + 1):
            close(part)
            both.append(bufs[part][...].reshape(4096, 128))
        total = jnp.dot(
            main_ref[...], jnp.concatenate(both, axis=1), preferred_element_type=jnp.float32
        )
        total = total + jnp.dot(
            tail_ref[...], jnp.concatenate(rest[first:first + 2], axis=1),
            preferred_element_type=jnp.float32,
        )
        half_ref[:, 128 * first:128 * first + 256] = total.astype(jnp.bfloat16)

    def regroup(number, from_hi):
        if number < 2:
            to_core = jnp.int32(number)
            src = half_ref.at[pl.ds(number * 128, 128)]
            dst = kv_ref.at[0, pl.ds(pl.multiple_of(from_hi * 128, 128), 128)]
        else:
            to_core = y_hi
            src = half_ref.at[pl.ds(256, 16)]
            dst = pool_ref.at[y_hi * 32 + pair]
        to = {**me, "y": core * 2 + y_lo, "core": to_core}
        stays = jnp.logical_and(core == y_hi, core == to_core)
        return src, dst, to, stays

    def regroup_send(number):
        src, dst, to, stays = regroup(number, y_hi)
        recv_sem = group_recv.at[y_hi] if number < 2 else group_recv.at[2]

        @pl.when(stays)
        def _():
            pltpu.make_async_copy(src, dst, recv_sem).start()

        @pl.when(jnp.logical_not(stays))
        def _():
            send(src, dst, group_send.at[number], recv_sem, to).start()

    for number in (2, 0, 1):
        regroup_send(number)
    query_out.start()

    def pool_copies(phase):
        if phase == 0:
            block, axis = pool_ref.at[pl.ds(core * 32 + pair, 1)], "z"
        else:
            block, axis = pool_ref.at[pl.ds(core * 32 + me["x"] * 8, 8)], "x"
        base = 0 if phase == 0 else SIZE["z"] - 1
        return [
            send(
                block, block, pool_send.at[base + by - 1], pool_recv.at[base + by - 1],
                moved(me, axis, by),
            )
            for by in range(1, SIZE[axis])
        ]

    half_pool = pool_ref.at[pl.ds(core * 32, 32)]
    pool_swap = send(half_pool, half_pool, pool_send.at[10], pool_recv.at[10], mate)

    def chunk(slot, number):
        return kv_ref.at[slot, pl.ds(number * CHUNK, CHUNK)]

    def forth(step, number):
        return send(
            chunk(slot_of(step - 1), number), chunk(slot_of(step), number),
            halo_send.at[step - 1, number], halo_recv.at[step - 1, number], along(me, 1),
        )

    def back(step, number):
        if step == 0:
            src, to = slot_of(0), moved(me, "x", 1)
        else:
            src, to = slot_of(9 - step), along(me, -1)
        return send(
            chunk(src, number), chunk(slot_of(8 - step), number),
            halo_send.at[4 + step, number], halo_recv.at[4 + step, number], to,
        )

    def own_arrives(from_hi):
        src = half_ref.at[pl.ds(0, 128)]
        dst = kv_ref.at[0, pl.ds(from_hi * 128, 128)]
        send(src, dst, group_send.at[0], group_recv.at[from_hi], mate).wait_recv()

    for from_hi in range(2):
        own_arrives(from_hi)
        for number in range(2 * from_hi, 2 * from_hi + 2):
            forth(1, number).start()
            back(0, number).start()
    page = pool_ref.at[core * 32 + pair]
    send(half_ref.at[pl.ds(256, 16)], page, group_send.at[2], group_recv.at[2], mate).wait_recv()
    for copy in pool_copies(0):
        copy.start()

    def attend(first, count, masked, at):
        rows = count * PAIR
        head = at // 5
        query = query_ref[:, :, at * 128:at * 128 + 128].reshape(PAIR, 128)
        key = kv_ref[first:first + count, :, head * 128:head * 128 + 128].reshape(rows, 128)
        value = kv_ref[first:first + count, :, 256 + head * 128:384 + head * 128]
        score = lax.dot_general(
            query, key, (((1,), (1,)), ((), ())), preferred_element_type=jnp.float32
        )
        if masked:
            score = score + bias_ref[:, :rows]
        old = top_ref[at]
        new = jnp.maximum(old, jnp.max(score, axis=1, keepdims=True))
        factor = jnp.exp2((old - new) * SCALE)
        weight = jnp.exp2((score - jnp.concatenate([new] * (rows // 128), axis=1)) * SCALE)
        part = weight[:, :128]
        for lanes in range(128, rows, 128):
            part = part + weight[:, lanes:lanes + 128]
        top_ref[at] = new
        total_ref[at] = total_ref[at] * factor + part
        sum_ref[at] = sum_ref[at] * factor + jnp.dot(
            weight.astype(jnp.bfloat16), value.reshape(rows, 128),
            preferred_element_type=jnp.float32,
        )

    def give(at):
        first = pl.multiple_of(y_hi * HALF_WIDTH + at * 128, 128)
        return send(
            give_ref.at[:, pl.ds(at * 128, 128)], out_ref.at[:, pl.ds(first, 128)],
            give_send.at[at], give_recv.at[at], partner,
        )

    def finish(at):
        total = jnp.sum(total_ref[at], axis=1, keepdims=True)
        done = (sum_ref[at] / total).astype(jnp.bfloat16).reshape(2, 128, 128)
        for hi in range(2):
            @pl.when(y_hi == hi)
            def _():
                first = hi * HALF_WIDTH + at * 128
                out_ref[:, first:first + 128] = done[hi]
                give_ref[:, at * 128:at * 128 + 128] = done[1 - hi]
        give(at).start()

    def stage(step):
        bias_ref[:, :PAIR] = bias_of(step)
        bias_ref[:, PAIR:] = bias_of(9 - step)

    def prompt_in():
        pool_swap.wait_recv()

        def page_in(number, carry):
            first = pl.multiple_of(lax.rem(number, 16) * 16, 16)
            at = table_ref[0, number]
            kv_ref[9 + lax.div(number, 16), pl.ds(first, 16)] = pool_ref[
                lax.rem(at, 2) * 32 + lax.div(at, 2)
            ]
            return carry

        lax.fori_loop(0, 32, page_in, 0)

    def heads(number, parts):
        return range(10 * number // parts, 10 * (number + 1) // parts)

    for step in range(1, 5):
        for number in range(CHUNKS):
            forth(step, number).wait_recv()
            if step < 4:
                forth(step + 1, number).start()
            back(step - 1, number).wait_recv()
            if step < 4:
                back(step, number).start()
            if step == 2 and number == 0:
                for copy in pool_copies(0):
                    copy.wait_recv()
                for copy in pool_copies(1):
                    copy.start()
            if step == 3 and number == 1:
                for copy in pool_copies(1):
                    copy.wait_recv()
                pool_swap.start()
            if step == 1:
                if number == CHUNKS // 2:
                    query_out.wait_recv()
                    query_stay.wait()
                if number >= CHUNKS // 2:
                    for at in heads(number - CHUNKS // 2, CHUNKS - CHUNKS // 2):
                        attend(0, 1, True, at)
            else:
                for at in heads(number, CHUNKS):
                    attend(2 * step - 3, 2, True, at)
            if step == 4:
                if number == 0:
                    prompt_in()
                for at in heads(number, CHUNKS):
                    attend(9, 2, False, at)
        stage(step)
    for at in range(10):
        attend(7, 2, True, at)
        finish(at)

    for at in range(10):
        give(at).wait()
    for copy in to_mate:
        copy.wait_send()
    rows_out.wait_send()
    query_out.wait_send()
    for part in range(PARTS):
        for phase in range(2):
            for copy in direct(part, phase):
                copy.wait_send()
        for step, way, half in ring_sends(part):
            ring(part, step, way, half).wait_send()
    for number in range(3):
        src, dst, to, stays = regroup(number, y_hi)

        @pl.when(jnp.logical_not(stays))
        def _():
            send(src, dst, group_send.at[number], group_recv.at[0], to).wait_send()

    for phase in range(2):
        for copy in pool_copies(phase):
            copy.wait_send()
    pool_swap.wait_send()
    for step in range(1, 5):
        for number in range(CHUNKS):
            forth(step, number).wait_send()
            back(step - 1, number).wait_send()


def body(hidden, queries, key_value_weight, pooled_hidden_states, group_page_table, resp_lengths):
    in_hbm = pl.BlockSpec(memory_space=pl.ANY)
    in_vmem = pl.BlockSpec(memory_space=pltpu.VMEM)
    in_smem = pl.BlockSpec(memory_space=pltpu.SMEM)
    dma = pltpu.SemaphoreType.DMA
    shards = pltpu.VMEM((2, 2, 4, 8, 2, 16, 128), jnp.bfloat16)
    sums = pltpu.VMEM((HALF_HEADS, PAIR, 128), jnp.float32)
    out = pl.pallas_call(
        kernel,
        name="attend",
        out_shape=jax.ShapeDtypeStruct((DEVICE_TOKENS, QUERY_HEADS * HEAD_SIZE), jnp.bfloat16),
        in_specs=[in_vmem, in_hbm, in_hbm, in_hbm, in_smem, in_smem],
        out_specs=in_vmem,
        scratch_shapes=[
            shards, shards, shards, shards, shards,
            pltpu.VMEM((2, 16, 128), jnp.bfloat16),
            pltpu.VMEM((ROWS, WIDTH), jnp.bfloat16),
            pltpu.VMEM((640, 640), jnp.bfloat16),
            pltpu.VMEM((ROWS, 4096), jnp.bfloat16),
            pltpu.VMEM((ROWS, 1024), jnp.bfloat16),
            pltpu.VMEM((4096, 128), jnp.float32),
            pltpu.VMEM((ROWS, 512), jnp.bfloat16),
            pltpu.VMEM((11, PAIR, 512), jnp.bfloat16),
            pltpu.VMEM((64, PAGE_TOKENS, 512), jnp.bfloat16),
            pltpu.VMEM((2, DEVICE_TOKENS, HALF_WIDTH), jnp.bfloat16),
            pltpu.VMEM((DEVICE_TOKENS, HALF_WIDTH), jnp.bfloat16),
            pltpu.VMEM((PAIR, 2 * PAIR), jnp.float32),
            pltpu.VMEM((PAIR, PAIR), jnp.int32),
            sums, sums, sums,
            dma((PARTS, 26)), dma((PARTS, 26)), dma((6,)), dma((6,)), dma((8,)),
            dma((3,)), dma((3,)), dma, dma,
            dma((8, CHUNKS)), dma((8, CHUNKS)), dma((11,)), dma((11,)),
            dma((HALF_HEADS,)), dma((HALF_HEADS,)),
        ],
        compiler_params=pltpu.CompilerParams(
            collective_id=0, has_side_effects=True, vmem_limit_bytes=56 * 1024 * 1024
        ),
    )(
        key_value_weight, hidden[0], pooled_hidden_states[0], queries[0],
        group_page_table, resp_lengths,
    )
    return out[None]


def solution(mesh):
    in_specs = (
        P("group", "ctx", None),
        P("group", "ctx", None),
        P(("group", "ctx"), None),
        P("ctx", None, None),
        P("group", None),
        P("group", None),
    )
    out_specs = P("group", "ctx", None)
    return jax.shard_map(body, mesh=mesh, in_specs=in_specs, out_specs=out_specs, check_vma=False)
```

```python
import math

import jax
import jax.numpy as jnp
from jax import lax
from jax.experimental import pallas as pl
from jax.experimental.pallas import tpu as pltpu
from jax.sharding import PartitionSpec as P

QUERY_HEADS = 20
KEY_VALUE_HEADS = 4
HEAD_SIZE = 128
DEVICE_TOKENS = 128
PAGE_TOKENS = 16
WIDTH = 5120
SCALE = math.log2(math.e) / math.sqrt(HEAD_SIZE)
HALF_HEADS = QUERY_HEADS // 2
HALF_WIDTH = HALF_HEADS * HEAD_SIZE
PAIR = 2 * DEVICE_TOKENS
ROW_CHUNKS = 2
CHUNKS = 2 * ROW_CHUNKS
CHUNK = PAIR // ROW_CHUNKS
ROWS = 2 * DEVICE_TOKENS + PAGE_TOKENS
SIZE = {"x": 4, "y": 4, "z": 8}
ORDERS = (("z", "x", "y"), ("z", "x", "y"), ("z", "y", "x"), ("z", "y", "x"), ("x", "y", "z"))
PARTS = len(ORDERS)


def place():
    g, c = lax.axis_index("group"), lax.axis_index("ctx")
    y_lo, core = lax.div(g, 2), lax.rem(g, 2)
    y_hi, z, x = lax.rem(c, 2), lax.rem(lax.div(c, 2), 8), lax.div(c, 16)
    return {"x": x, "y": y_hi * 2 + y_lo, "z": z, "core": core}


def device(at):
    return (
        lax.rem(at["y"], 2) * 2 + at["core"],
        (at["x"] * 8 + at["z"]) * 2 + lax.div(at["y"], 2),
    )


def moved(at, axis, by):
    there = dict(at)
    there[axis] = lax.rem(at[axis] + (by + SIZE[axis]), SIZE[axis])
    return there


def other_core(at):
    return {**at, "core": 1 - at["core"]}


def send(src, dst, send_sem, recv_sem, at):
    return pltpu.make_async_remote_copy(
        src_ref=src,
        dst_ref=dst,
        send_sem=send_sem,
        recv_sem=recv_sem,
        device_id=device(at),
        device_id_type=pl.DeviceIdType.MESH,
    )


def ring_block(buf, me, axis, done, position, half):
    def pick(name):
        if name == axis:
            return position
        return None if name in done else me[name]

    x, y, z = pick("x"), pick("y"), pick("z")
    everything = slice(None)
    y_lo = everything if y is None else lax.rem(y, 2)
    y_hi = everything if y is None else lax.div(y, 2)
    core = everything if half is None else half
    return buf.at[
        y_lo, core, everything if x is None else x, everything if z is None else z, y_hi
    ]


def along(me, by):
    at = lax.rem(me["x"] * 8 + me["z"] + (32 + by), 32)
    return {**me, "x": lax.div(at, 8), "z": lax.rem(at, 8)}


def slot_of(back):
    return 0 if back == 0 else 2 * back - 1 if back <= 4 else 2 * (9 - back)


def kernel(
    w_ref, hidden_ref, pages_in_ref, queries_ref, table_ref, lengths_ref, out_ref,
    ga, gb, gc, gd, ge, rem_ref, rows_ref, perm_ref, main_ref, tail_ref, wide_ref, half_ref,
    kv_ref, pool_ref, query_ref, give_ref, bias_ref, begin_ref, top_ref, total_ref, sum_ref,
    weight_send, weight_recv, mate_send, mate_recv, local_sem,
    group_send, group_recv, query_send, query_recv,
    halo_send, halo_recv, pool_send, pool_recv, give_send, give_recv,
):
    me = place()
    core = me["core"]
    mate = other_core(me)
    y_lo, y_hi = lax.rem(me["y"], 2), lax.div(me["y"], 2)
    pair = me["x"] * 8 + me["z"]
    partner = moved(me, "y", 2)
    neighbours = [mate, other_core(partner), along(me, 1), along(me, -1)] + [
        moved(me, axis, by) for axis in "xyz" for by in range(1, SIZE[axis])
    ]
    barrier = pltpu.get_barrier_semaphore()
    for at in neighbours:
        pl.semaphore_signal(
            barrier, inc=1, device_id=device(at), device_id_type=pl.DeviceIdType.MESH
        )

    own_rows = pl.ds(pl.multiple_of(core * 128, 128), 128)
    rows_stay = pltpu.make_async_copy(hidden_ref, rows_ref.at[own_rows], local_sem.at[5])
    pool_stay = pltpu.make_async_copy(pages_in_ref, rows_ref.at[pl.ds(256, 16)], local_sem.at[6])
    rows_stay.start()
    pool_stay.start()
    rest = w_ref[16:20, :].astype(jnp.float32)
    for half in range(2):
        pieces = []
        for row in range(4):
            for block in range(4):
                first = (block // 2) * 512 + half * 256 + (block % 2) * 128
                pieces.append(rest[row:row + 1, first:first + 128])
        rem_ref[half] = jnp.concatenate(pieces, axis=0).astype(jnp.bfloat16)
    row = lax.broadcasted_iota(jnp.int32, (640, 640), 0)
    col = lax.broadcasted_iota(jnp.int32, (640, 640), 1)
    last = col - 512
    source = jnp.where(
        col < 512,
        20 * lax.shift_right_logical(col, 4) + (col & 15),
        20 * lax.shift_right_logical(last, 2) + 16 + (last & 3),
    )
    perm_ref[...] = jnp.where(row == source, 1.0, 0.0).astype(jnp.bfloat16)
    pl.semaphore_wait(barrier, len(neighbours))

    bufs = (ga, gb, gc, gd, ge)

    def slot(buf, of_core):
        return buf.at[y_lo, of_core, me["x"], me["z"], y_hi]

    def shard_parts(half):
        starts = (half * 256, half * 256 + 128, half * 256 + 512, half * 256 + 640)
        return [
            w_ref.at[pl.ds(0, 16), pl.ds(pl.multiple_of(start, 128), 128)] for start in starts
        ] + [rem_ref.at[half]]

    to_mate = [
        send(src, slot(buf, core), mate_send.at[n], mate_recv.at[n], mate)
        for n, (src, buf) in enumerate(zip(shard_parts(1 - core), bufs))
    ]
    stay = [
        pltpu.make_async_copy(src, slot(buf, core), local_sem.at[n])
        for n, (src, buf) in enumerate(zip(shard_parts(core), bufs))
    ]
    for copy in to_mate + stay:
        copy.start()

    def direct(part, phase):
        order = ORDERS[part]
        axis, done = order[phase], order[:phase]
        base = 0 if phase == 0 else SIZE[order[0]] - 1
        block = ring_block(bufs[part], me, axis, done, me[axis], None)
        return [
            send(
                block, block, weight_send.at[part, base + by - 1],
                weight_recv.at[part, base + by - 1], moved(me, axis, by),
            )
            for by in range(1, SIZE[axis])
        ]

    def ring(part, step, way, half):
        order = ORDERS[part]
        axis, size = order[2], SIZE[order[2]]
        sign = 1 - 2 * way
        index = SIZE[order[0]] + SIZE[order[1]] - 2 + ((step - 1) * 2 + way) * 2 + half
        at = lax.rem(me[axis] + (size - sign * (step - 1)), size)
        block = ring_block(bufs[part], me, axis, order[:2], at, half)
        return send(
            block, block, weight_send.at[part, index], weight_recv.at[part, index],
            moved(me, axis, sign),
        )

    def ring_steps(part):
        return SIZE[ORDERS[part][2]] // 2

    def ring_sends(part):
        steps = ring_steps(part)
        return [
            (step, way, half)
            for step in range(1, steps + 1) for way in range(2) for half in range(2)
            if step < steps or half == way
        ]

    def second(part):
        for copy in direct(part, 0):
            copy.wait_recv()
        for copy in direct(part, 1):
            copy.start()

    def third(part):
        for copy in direct(part, 1):
            copy.wait_recv()
        for turn in range(2):
            for way in range(2):
                ring(part, 1, way, way ^ turn).start()

    def pass_on(part, step, turn):
        for way in range(2):
            ring(part, step, way, way ^ turn).wait_recv()
            if step + 1 < ring_steps(part) or turn == 0:
                ring(part, step + 1, way, way ^ turn).start()

    def close(part):
        steps = ring_steps(part)
        for way in range(2):
            ring(part, steps - 1, way, 1 - way).wait_recv()
        for way in range(2):
            ring(part, steps, way, way).wait_recv()

    for part in (4, 0, 2, 1, 3):
        to_mate[part].wait_recv()
        stay[part].wait()
        for copy in direct(part, 0):
            copy.start()
    rows_out = send(hidden_ref, rows_ref.at[own_rows], mate_send.at[5], mate_recv.at[5], mate)
    rows_out.start()

    def half_columns(ref, of):
        return ref.at[:, pl.ds(pl.multiple_of(of * HALF_WIDTH, 128), HALF_WIDTH)]

    query_out = send(
        half_columns(queries_ref, 1 - y_hi), query_ref.at[y_hi], query_send, query_recv, partner
    )
    query_stay = pltpu.make_async_copy(
        half_columns(queries_ref, y_hi), query_ref.at[y_hi], local_sem.at[7]
    )
    query_stay.start()

    def reorder(first, count):
        def one(number, carry):
            block = rows_ref[:, pl.ds(pl.multiple_of(number * 640, 128), 640)]
            turned = jnp.dot(block, perm_ref[...], preferred_element_type=jnp.float32)
            turned = turned.astype(jnp.bfloat16)
            main_ref[:, pl.ds(pl.multiple_of(number * 512, 128), 512)] = turned[:, :512]
            tail_ref[:, pl.ds(pl.multiple_of(number * 128, 128), 128)] = turned[:, 512:]
            return carry

        lax.fori_loop(first, first + count, one, 0)

    second(4)
    second(0)
    second(2)
    rows_stay.wait()
    pool_stay.wait()
    third(4)
    second(1)
    second(3)
    pass_on(4, 1, 0)
    pass_on(4, 1, 1)
    third(0)
    third(2)
    rows_out.wait_recv()
    reorder(0, 2)
    pass_on(4, 2, 0)
    third(1)
    third(3)
    pass_on(4, 2, 1)
    reorder(2, 2)
    pass_on(0, 1, 0)
    pass_on(2, 1, 0)
    pass_on(4, 3, 0)
    reorder(4, 2)
    pass_on(1, 1, 0)
    pass_on(3, 1, 0)
    reorder(6, 2)

    token = lax.broadcasted_iota(jnp.int32, (PAIR, PAIR), 0)
    lane = lax.broadcasted_iota(jnp.int32, (PAIR, PAIR), 1)
    position = pair * PAIR + token
    begin = jnp.zeros((PAIR, PAIR), jnp.int32)
    end = jnp.int32(0)
    for number in range(8):
        end = end + lengths_ref[0, number]
        begin = jnp.where(position >= end, end, begin)
    begin_ref[...] = begin
    top_ref[...] = jnp.full(top_ref.shape, -jnp.inf, jnp.float32)
    total_ref[...] = jnp.zeros(total_ref.shape, jnp.float32)
    sum_ref[...] = jnp.zeros(sum_ref.shape, jnp.float32)

    def bias_of(back_by):
        key = (pair - back_by) * PAIR + lane
        live = key >= begin_ref[...]
        if back_by == 0:
            live = jnp.logical_and(live, key <= position)
        return jnp.where(live, 0.0, -jnp.inf).astype(jnp.float32)

    bias_ref[:, :PAIR] = bias_of(0)

    close(4)
    wide_ref[...] = ge[...].reshape(4096, 128).astype(jnp.float32)
    rest = [
        wide_ref[pl.ds(block, 1024, stride=4), :].astype(jnp.bfloat16) for block in range(4)
    ]
    for first in (0, 2):
        both = []
        for part in (first, first + 1):
            close(part)
            both.append(bufs[part][...].reshape(4096, 128))
        total = jnp.dot(
            main_ref[...], jnp.concatenate(both, axis=1), preferred_element_type=jnp.float32
        )
        total = total + jnp.dot(
            tail_ref[...], jnp.concatenate(rest[first:first + 2], axis=1),
            preferred_element_type=jnp.float32,
        )
        total = total.astype(jnp.bfloat16)
        for head in range(2):
            half_ref[head, :, 64 * first:64 * first + 128] = total[:, 128 * head:128 * head + 128]

    def regroup(number, from_hi):
        if number < 4:
            head, to_core = number // 2, jnp.int32(number % 2)
            src = half_ref.at[head, pl.ds((number % 2) * 128, 128)]
            dst = kv_ref.at[head, 0, pl.ds(pl.multiple_of(from_hi * 128, 128), 128)]
            recv_sem = group_recv.at[head, from_hi]
        else:
            to_core = y_hi
            src = half_ref.at[y_lo, pl.ds(256, 16)]
            dst = pool_ref.at[y_hi * 32 + pair, y_lo]
            recv_sem = group_recv.at[2, 0]
        to = {**me, "y": core * 2 + y_lo, "core": to_core}
        stays = jnp.logical_and(core == y_hi, core == to_core)
        return src, dst, recv_sem, to, stays

    def regroup_send(number):
        src, dst, recv_sem, to, stays = regroup(number, y_hi)

        @pl.when(stays)
        def _():
            pltpu.make_async_copy(src, dst, recv_sem).start()

        @pl.when(jnp.logical_not(stays))
        def _():
            send(src, dst, group_send.at[number], recv_sem, to).start()

    for number in range(5):
        regroup_send(number)
    query_out.start()

    def pool_copies(phase):
        if phase == 0:
            block, axis = pool_ref.at[pl.ds(core * 32 + pair, 1), y_lo], "z"
        else:
            block, axis = pool_ref.at[pl.ds(core * 32 + me["x"] * 8, 8), y_lo], "x"
        base = 0 if phase == 0 else SIZE["z"] - 1
        return [
            send(
                block, block, pool_send.at[base + by - 1], pool_recv.at[base + by - 1],
                moved(me, axis, by),
            )
            for by in range(1, SIZE[axis])
        ]

    one_head = pool_ref.at[pl.ds(core * 32, 32), y_lo]
    pool_heads = send(
        one_head, one_head, pool_send.at[10], pool_recv.at[10],
        {**me, "y": y_hi * 2 + 1 - y_lo},
    )
    half_pool = pool_ref.at[pl.ds(core * 32, 32)]
    pool_swap = send(half_pool, half_pool, pool_send.at[11], pool_recv.at[11], mate)

    def chunk(slot, number):
        head, part = number % 2, number // 2
        return kv_ref.at[head, slot, pl.ds(part * CHUNK, CHUNK)]

    def forth(step, number):
        return send(
            chunk(slot_of(step - 1), number), chunk(slot_of(step), number),
            halo_send.at[step - 1, number], halo_recv.at[step - 1, number], along(me, 1),
        )

    def back(step, number):
        if step == 0:
            src, to = slot_of(0), moved(me, "x", 1)
        else:
            src, to = slot_of(9 - step), along(me, -1)
        return send(
            chunk(src, number), chunk(slot_of(8 - step), number),
            halo_send.at[4 + step, number], halo_recv.at[4 + step, number], to,
        )

    for number in range(CHUNKS):
        head, from_hi = number % 2, number // 2
        src = half_ref.at[head, pl.ds(0, 128)]
        dst = kv_ref.at[head, 0, pl.ds(from_hi * 128, 128)]
        send(src, dst, group_send.at[head], group_recv.at[head, from_hi], mate).wait_recv()
        forth(1, number).start()
        back(0, number).start()
    page = pool_ref.at[core * 32 + pair, y_lo]
    page_here = half_ref.at[y_lo, pl.ds(256, 16)]
    send(page_here, page, group_send.at[4], group_recv.at[2, 0], mate).wait_recv()
    for copy in pool_copies(0):
        copy.start()

    def attend(first, count, masked, at):
        rows = count * PAIR
        head = at // 5
        query = query_ref[:, :, at * 128:at * 128 + 128].reshape(PAIR, 128)
        key = kv_ref[head, first:first + count, :, :128].reshape(rows, 128)
        value = kv_ref[head, first:first + count, :, 128:]
        score = lax.dot_general(
            query, key, (((1,), (1,)), ((), ())), preferred_element_type=jnp.float32
        )
        if masked:
            score = score + bias_ref[:, :rows]
        old = top_ref[at]
        new = jnp.maximum(old, jnp.max(score, axis=1, keepdims=True))
        factor = jnp.exp2((old - new) * SCALE)
        weight = jnp.exp2((score - jnp.concatenate([new] * (rows // 128), axis=1)) * SCALE)
        part = weight[:, :128]
        for lanes in range(128, rows, 128):
            part = part + weight[:, lanes:lanes + 128]
        top_ref[at] = new
        total_ref[at] = total_ref[at] * factor + part
        sum_ref[at] = sum_ref[at] * factor + jnp.dot(
            weight.astype(jnp.bfloat16), value.reshape(rows, 128),
            preferred_element_type=jnp.float32,
        )

    def give(at):
        first = pl.multiple_of(y_hi * HALF_WIDTH + at * 128, 128)
        return send(
            give_ref.at[:, pl.ds(at * 128, 128)], out_ref.at[:, pl.ds(first, 128)],
            give_send.at[at], give_recv.at[at], partner,
        )

    def finish(at):
        total = jnp.sum(total_ref[at], axis=1, keepdims=True)
        done = (sum_ref[at] / total).astype(jnp.bfloat16).reshape(2, 128, 128)
        for hi in range(2):
            @pl.when(y_hi == hi)
            def _():
                first = hi * HALF_WIDTH + at * 128
                out_ref[:, first:first + 128] = done[hi]
                give_ref[:, at * 128:at * 128 + 128] = done[1 - hi]
        give(at).start()

    def stage(step):
        bias_ref[:, :PAIR] = bias_of(step)
        bias_ref[:, PAIR:] = bias_of(9 - step)

    def prompt_in():
        pool_swap.wait_recv()

        def page_in(number, carry):
            first = pl.multiple_of(lax.rem(number, 16) * 16, 16)
            at = table_ref[0, number]
            rows = pool_ref[lax.rem(at, 2) * 32 + lax.div(at, 2)]
            for head in range(2):
                kv_ref[head, 9 + lax.div(number, 16), pl.ds(first, 16)] = rows[head]
            return carry

        lax.fori_loop(0, 32, page_in, 0)

    def heads(number, parts):
        return range(10 * number // parts, 10 * (number + 1) // parts)

    for step in range(1, 4):
        for number in range(CHUNKS):
            back(step - 1, number).wait_recv()
            back(step, number).start()
            forth(step, number).wait_recv()
            forth(step + 1, number).start()
            if step == 2 and number == 0:
                for copy in pool_copies(0):
                    copy.wait_recv()
                for copy in pool_copies(1):
                    copy.start()
            if step == 1 and number == 2:
                query_out.wait_recv()
                query_stay.wait()
            if step == 3 and number == 0:
                for copy in pool_copies(1):
                    copy.wait_recv()
                pool_heads.start()
            if step == 3 and number == 3:
                pool_heads.wait_recv()
                pool_swap.start()
            if step > 1:
                for at in heads(number, CHUNKS):
                    attend(2 * step - 3, 2, True, at)
            elif number >= CHUNKS // 2:
                for at in heads(number - CHUNKS // 2, CHUNKS - CHUNKS // 2):
                    attend(0, 1, True, at)
        stage(step)
    for at in range(10):
        attend(5, 2, True, at)
    stage(4)
    prompt_in()
    for head in range(2):
        for at in range(5 * head, 5 * head + 5):
            attend(9, 2, False, at)
        for number in range(head, CHUNKS, 2):
            forth(4, number).wait_recv()
            back(3, number).wait_recv()
        for at in range(5 * head, 5 * head + 5):
            attend(7, 2, True, at)
            finish(at)

    for at in range(10):
        give(at).wait()
    for copy in to_mate:
        copy.wait_send()
    rows_out.wait_send()
    query_out.wait_send()
    for part in range(PARTS):
        for phase in range(2):
            for copy in direct(part, phase):
                copy.wait_send()
        for step, way, half in ring_sends(part):
            ring(part, step, way, half).wait_send()
    for number in range(5):
        src, dst, recv_sem, to, stays = regroup(number, y_hi)

        @pl.when(jnp.logical_not(stays))
        def _():
            send(src, dst, group_send.at[number], recv_sem, to).wait_send()

    for phase in range(2):
        for copy in pool_copies(phase):
            copy.wait_send()
    pool_heads.wait_send()
    pool_swap.wait_send()
    for step in range(1, 5):
        for number in range(CHUNKS):
            forth(step, number).wait_send()
            back(step - 1, number).wait_send()


def body(hidden, queries, key_value_weight, pooled_hidden_states, group_page_table, resp_lengths):
    in_hbm = pl.BlockSpec(memory_space=pl.ANY)
    in_vmem = pl.BlockSpec(memory_space=pltpu.VMEM)
    in_smem = pl.BlockSpec(memory_space=pltpu.SMEM)
    dma = pltpu.SemaphoreType.DMA
    shards = pltpu.VMEM((2, 2, 4, 8, 2, 16, 128), jnp.bfloat16)
    sums = pltpu.VMEM((HALF_HEADS, PAIR, 128), jnp.float32)
    out = pl.pallas_call(
        kernel,
        name="attend",
        out_shape=jax.ShapeDtypeStruct((DEVICE_TOKENS, QUERY_HEADS * HEAD_SIZE), jnp.bfloat16),
        in_specs=[in_vmem, in_hbm, in_hbm, in_hbm, in_smem, in_smem],
        out_specs=in_vmem,
        scratch_shapes=[
            shards, shards, shards, shards, shards,
            pltpu.VMEM((2, 16, 128), jnp.bfloat16),
            pltpu.VMEM((ROWS, WIDTH), jnp.bfloat16),
            pltpu.VMEM((640, 640), jnp.bfloat16),
            pltpu.VMEM((ROWS, 4096), jnp.bfloat16),
            pltpu.VMEM((ROWS, 1024), jnp.bfloat16),
            pltpu.VMEM((4096, 128), jnp.float32),
            pltpu.VMEM((2, ROWS, 256), jnp.bfloat16),
            pltpu.VMEM((2, 11, PAIR, 256), jnp.bfloat16),
            pltpu.VMEM((64, 2, PAGE_TOKENS, 256), jnp.bfloat16),
            pltpu.VMEM((2, DEVICE_TOKENS, HALF_WIDTH), jnp.bfloat16),
            pltpu.VMEM((DEVICE_TOKENS, HALF_WIDTH), jnp.bfloat16),
            pltpu.VMEM((PAIR, 2 * PAIR), jnp.float32),
            pltpu.VMEM((PAIR, PAIR), jnp.int32),
            sums, sums, sums,
            dma((PARTS, 26)), dma((PARTS, 26)), dma((6,)), dma((6,)), dma((8,)),
            dma((5,)), dma((3, 2)), dma, dma,
            dma((8, CHUNKS)), dma((8, CHUNKS)), dma((12,)), dma((12,)),
            dma((HALF_HEADS,)), dma((HALF_HEADS,)),
        ],
        compiler_params=pltpu.CompilerParams(
            collective_id=0, has_side_effects=True, vmem_limit_bytes=56 * 1024 * 1024
        ),
    )(
        key_value_weight, hidden[0], pooled_hidden_states[0], queries[0],
        group_page_table, resp_lengths,
    )
    return out[None]


def solution(mesh):
    in_specs = (
        P("group", "ctx", None),
        P("group", "ctx", None),
        P(("group", "ctx"), None),
        P("ctx", None, None),
        P("group", None),
        P("group", None),
    )
    out_specs = P("group", "ctx", None)
    return jax.shard_map(body, mesh=mesh, in_specs=in_specs, out_specs=out_specs, check_vma=False)
```

```python
import math

import jax
import jax.numpy as jnp
from jax import lax
from jax.experimental import pallas as pl
from jax.experimental.pallas import tpu as pltpu
from jax.sharding import PartitionSpec as P

QUERY_HEADS = 20
KEY_VALUE_HEADS = 4
HEAD_SIZE = 128
DEVICE_TOKENS = 128
PAGE_TOKENS = 16
WIDTH = 5120
SCALE = math.log2(math.e) / math.sqrt(HEAD_SIZE)
HALF_HEADS = QUERY_HEADS // 2
HALF_WIDTH = HALF_HEADS * HEAD_SIZE
PAIR = 2 * DEVICE_TOKENS
CHUNKS = 4
CHUNK = PAIR // CHUNKS
ROWS = 2 * DEVICE_TOKENS + PAGE_TOKENS
SIZE = {"x": 4, "y": 4, "z": 8}
ORDERS = (("z", "x", "y"), ("z", "x", "y"), ("z", "y", "x"), ("z", "y", "x"), ("x", "y", "z"))
PARTS = len(ORDERS)


def place():
    g, c = lax.axis_index("group"), lax.axis_index("ctx")
    y_lo, core = lax.div(g, 2), lax.rem(g, 2)
    y_hi, z, x = lax.rem(c, 2), lax.rem(lax.div(c, 2), 8), lax.div(c, 16)
    return {"x": x, "y": y_hi * 2 + y_lo, "z": z, "core": core}


def device(at):
    return (
        lax.rem(at["y"], 2) * 2 + at["core"],
        (at["x"] * 8 + at["z"]) * 2 + lax.div(at["y"], 2),
    )


def moved(at, axis, by):
    there = dict(at)
    there[axis] = lax.rem(at[axis] + (by + SIZE[axis]), SIZE[axis])
    return there


def other_core(at):
    return {**at, "core": 1 - at["core"]}


def send(src, dst, send_sem, recv_sem, at):
    return pltpu.make_async_remote_copy(
        src_ref=src,
        dst_ref=dst,
        send_sem=send_sem,
        recv_sem=recv_sem,
        device_id=device(at),
        device_id_type=pl.DeviceIdType.MESH,
    )


def ring_block(buf, me, axis, done, position, half):
    def pick(name):
        if name == axis:
            return position
        return None if name in done else me[name]

    x, y, z = pick("x"), pick("y"), pick("z")
    everything = slice(None)
    y_lo = everything if y is None else lax.rem(y, 2)
    y_hi = everything if y is None else lax.div(y, 2)
    core = everything if half is None else half
    return buf.at[
        y_lo, core, everything if x is None else x, everything if z is None else z, y_hi
    ]


def along(me, by):
    at = lax.rem(me["x"] * 8 + me["z"] + (32 + by), 32)
    return {**me, "x": lax.div(at, 8), "z": lax.rem(at, 8)}


def slot_of(back):
    return 0 if back == 0 else 2 * back - 1 if back <= 4 else 2 * (9 - back)


def kernel(
    w_ref, hidden_ref, pages_in_ref, queries_ref, table_ref, lengths_ref, out_ref,
    ga, gb, gc, gd, ge, rem_ref, rows_ref, perm_ref, main_ref, tail_ref, wide_ref, half_ref,
    kv_ref, pool_ref, query_ref, give_ref, bias_ref, begin_ref, top_ref, total_ref, sum_ref,
    weight_send, weight_recv, mate_send, mate_recv, local_sem,
    group_send, group_recv, query_send, query_recv,
    halo_send, halo_recv, pool_send, pool_recv, give_send, give_recv,
):
    me = place()
    core = me["core"]
    mate = other_core(me)
    y_lo, y_hi = lax.rem(me["y"], 2), lax.div(me["y"], 2)
    pair = me["x"] * 8 + me["z"]
    partner = moved(me, "y", 2)
    neighbours = [mate, other_core(partner), along(me, 1), along(me, -1)] + [
        moved(me, axis, by) for axis in "xyz" for by in range(1, SIZE[axis])
    ]
    barrier = pltpu.get_barrier_semaphore()
    for at in neighbours:
        pl.semaphore_signal(
            barrier, inc=1, device_id=device(at), device_id_type=pl.DeviceIdType.MESH
        )

    own_rows = pl.ds(pl.multiple_of(core * 128, 128), 128)
    rows_stay = pltpu.make_async_copy(hidden_ref, rows_ref.at[own_rows], local_sem.at[5])
    pool_stay = pltpu.make_async_copy(pages_in_ref, rows_ref.at[pl.ds(256, 16)], local_sem.at[6])
    rows_stay.start()
    pool_stay.start()
    rest = w_ref[16:20, :].astype(jnp.float32)
    for half in range(2):
        pieces = []
        for row in range(4):
            for block in range(4):
                first = (block // 2) * 512 + half * 256 + (block % 2) * 128
                pieces.append(rest[row:row + 1, first:first + 128])
        rem_ref[half] = jnp.concatenate(pieces, axis=0).astype(jnp.bfloat16)
    row = lax.broadcasted_iota(jnp.int32, (640, 640), 0)
    col = lax.broadcasted_iota(jnp.int32, (640, 640), 1)
    last = col - 512
    source = jnp.where(
        col < 512,
        20 * lax.shift_right_logical(col, 4) + (col & 15),
        20 * lax.shift_right_logical(last, 2) + 16 + (last & 3),
    )
    perm_ref[...] = jnp.where(row == source, 1.0, 0.0).astype(jnp.bfloat16)
    pl.semaphore_wait(barrier, len(neighbours))

    bufs = (ga, gb, gc, gd, ge)

    def slot(buf, of_core):
        return buf.at[y_lo, of_core, me["x"], me["z"], y_hi]

    def shard_parts(half):
        starts = (half * 256, half * 256 + 128, half * 256 + 512, half * 256 + 640)
        return [
            w_ref.at[pl.ds(0, 16), pl.ds(pl.multiple_of(start, 128), 128)] for start in starts
        ] + [rem_ref.at[half]]

    to_mate = [
        send(src, slot(buf, core), mate_send.at[n], mate_recv.at[n], mate)
        for n, (src, buf) in enumerate(zip(shard_parts(1 - core), bufs))
    ]
    stay = [
        pltpu.make_async_copy(src, slot(buf, core), local_sem.at[n])
        for n, (src, buf) in enumerate(zip(shard_parts(core), bufs))
    ]
    for copy in to_mate + stay:
        copy.start()

    def direct(part, phase):
        order = ORDERS[part]
        axis, done = order[phase], order[:phase]
        base = 0 if phase == 0 else SIZE[order[0]] - 1
        block = ring_block(bufs[part], me, axis, done, me[axis], None)
        return [
            send(
                block, block, weight_send.at[part, base + by - 1],
                weight_recv.at[part, base + by - 1], moved(me, axis, by),
            )
            for by in range(1, SIZE[axis])
        ]

    def ring(part, step, way, half):
        order = ORDERS[part]
        axis, size = order[2], SIZE[order[2]]
        sign = 1 - 2 * way
        index = SIZE[order[0]] + SIZE[order[1]] - 2 + ((step - 1) * 2 + way) * 2 + half
        at = lax.rem(me[axis] + (size - sign * (step - 1)), size)
        block = ring_block(bufs[part], me, axis, order[:2], at, half)
        return send(
            block, block, weight_send.at[part, index], weight_recv.at[part, index],
            moved(me, axis, sign),
        )

    def ring_steps(part):
        return SIZE[ORDERS[part][2]] // 2

    def ring_sends(part):
        steps = ring_steps(part)
        return [
            (step, way, half)
            for step in range(1, steps + 1) for way in range(2) for half in range(2)
            if step < steps or half == way
        ]

    def second(part):
        for copy in direct(part, 0):
            copy.wait_recv()
        for copy in direct(part, 1):
            copy.start()

    def third(part):
        for copy in direct(part, 1):
            copy.wait_recv()
        for turn in range(2):
            for way in range(2):
                ring(part, 1, way, way ^ turn).start()

    def pass_on(part, step, turn):
        for way in range(2):
            ring(part, step, way, way ^ turn).wait_recv()
            if step + 1 < ring_steps(part) or turn == 0:
                ring(part, step + 1, way, way ^ turn).start()

    def close(part):
        steps = ring_steps(part)
        for way in range(2):
            ring(part, steps - 1, way, 1 - way).wait_recv()
        for way in range(2):
            ring(part, steps, way, way).wait_recv()

    for part in (4, 0, 2, 1, 3):
        to_mate[part].wait_recv()
        stay[part].wait()
        for copy in direct(part, 0):
            copy.start()
    rows_out = send(hidden_ref, rows_ref.at[own_rows], mate_send.at[5], mate_recv.at[5], mate)
    rows_out.start()

    def half_columns(ref, of):
        return ref.at[:, pl.ds(pl.multiple_of(of * HALF_WIDTH, 128), HALF_WIDTH)]

    query_out = send(
        half_columns(queries_ref, 1 - y_hi), query_ref.at[y_hi], query_send, query_recv, partner
    )
    query_stay = pltpu.make_async_copy(
        half_columns(queries_ref, y_hi), query_ref.at[y_hi], local_sem.at[7]
    )
    query_stay.start()

    def reorder(first, count):
        def one(number, carry):
            block = rows_ref[:, pl.ds(pl.multiple_of(number * 640, 128), 640)]
            turned = jnp.dot(block, perm_ref[...], preferred_element_type=jnp.float32)
            turned = turned.astype(jnp.bfloat16)
            main_ref[:, pl.ds(pl.multiple_of(number * 512, 128), 512)] = turned[:, :512]
            tail_ref[:, pl.ds(pl.multiple_of(number * 128, 128), 128)] = turned[:, 512:]
            return carry

        lax.fori_loop(first, first + count, one, 0)

    second(4)
    second(0)
    second(2)
    rows_stay.wait()
    pool_stay.wait()
    third(4)
    second(1)
    second(3)
    pass_on(4, 1, 0)
    pass_on(4, 1, 1)
    third(0)
    third(2)
    rows_out.wait_recv()
    reorder(0, 2)
    pass_on(4, 2, 0)
    third(1)
    third(3)
    pass_on(4, 2, 1)
    reorder(2, 2)
    pass_on(0, 1, 0)
    pass_on(2, 1, 0)
    pass_on(4, 3, 0)
    reorder(4, 2)
    pass_on(1, 1, 0)
    pass_on(3, 1, 0)
    reorder(6, 2)

    token = lax.broadcasted_iota(jnp.int32, (PAIR, PAIR), 0)
    lane = lax.broadcasted_iota(jnp.int32, (PAIR, PAIR), 1)
    position = pair * PAIR + token
    begin = jnp.zeros((PAIR, PAIR), jnp.int32)
    end = jnp.int32(0)
    for number in range(8):
        end = end + lengths_ref[0, number]
        begin = jnp.where(position >= end, end, begin)
    begin_ref[...] = begin
    top_ref[...] = jnp.full(top_ref.shape, -jnp.inf, jnp.float32)
    total_ref[...] = jnp.zeros(total_ref.shape, jnp.float32)
    sum_ref[...] = jnp.zeros(sum_ref.shape, jnp.float32)

    def bias_of(back_by):
        key = (pair - back_by) * PAIR + lane
        live = key >= begin_ref[...]
        if back_by == 0:
            live = jnp.logical_and(live, key <= position)
        return jnp.where(live, 0.0, -jnp.inf).astype(jnp.float32)

    bias_ref[:, :PAIR] = bias_of(0)

    close(4)
    wide_ref[...] = ge[...].reshape(4096, 128).astype(jnp.float32)
    rest = [
        wide_ref[pl.ds(block, 1024, stride=4), :].astype(jnp.bfloat16) for block in range(4)
    ]
    for first in (0, 2):
        both = []
        for part in (first, first + 1):
            close(part)
            both.append(bufs[part][...].reshape(4096, 128))
        total = jnp.dot(
            main_ref[...], jnp.concatenate(both, axis=1), preferred_element_type=jnp.float32
        )
        total = total + jnp.dot(
            tail_ref[...], jnp.concatenate(rest[first:first + 2], axis=1),
            preferred_element_type=jnp.float32,
        )
        half_ref[:, 128 * first:128 * first + 256] = total.astype(jnp.bfloat16)

    def regroup(number, from_hi):
        if number < 2:
            to_core = jnp.int32(number)
            src = half_ref.at[pl.ds(number * 128, 128)]
            dst = kv_ref.at[0, pl.ds(pl.multiple_of(from_hi * 128, 128), 128)]
        else:
            to_core = y_hi
            src = half_ref.at[pl.ds(256, 16)]
            dst = pool_ref.at[y_hi * 32 + pair]
        to = {**me, "y": core * 2 + y_lo, "core": to_core}
        stays = jnp.logical_and(core == y_hi, core == to_core)
        return src, dst, to, stays

    def regroup_send(number):
        src, dst, to, stays = regroup(number, y_hi)
        recv_sem = group_recv.at[y_hi] if number < 2 else group_recv.at[2]

        @pl.when(stays)
        def _():
            pltpu.make_async_copy(src, dst, recv_sem).start()

        @pl.when(jnp.logical_not(stays))
        def _():
            send(src, dst, group_send.at[number], recv_sem, to).start()

    for number in (2, 0, 1):
        regroup_send(number)
    query_out.start()

    def pool_copies(phase):
        if phase == 0:
            block, axis = pool_ref.at[pl.ds(core * 32 + pair, 1)], "z"
        else:
            block, axis = pool_ref.at[pl.ds(core * 32 + me["x"] * 8, 8)], "x"
        base = 0 if phase == 0 else SIZE["z"] - 1
        return [
            send(
                block, block, pool_send.at[base + by - 1], pool_recv.at[base + by - 1],
                moved(me, axis, by),
            )
            for by in range(1, SIZE[axis])
        ]

    half_pool = pool_ref.at[pl.ds(core * 32, 32)]
    pool_swap = send(half_pool, half_pool, pool_send.at[10], pool_recv.at[10], mate)

    def chunk(slot, number):
        return kv_ref.at[slot, pl.ds(number * CHUNK, CHUNK)]

    def forth(step, number):
        return send(
            chunk(slot_of(step - 1), number), chunk(slot_of(step), number),
            halo_send.at[step - 1, number], halo_recv.at[step - 1, number], along(me, 1),
        )

    def back(step, number):
        if step == 0:
            src, to = slot_of(0), moved(me, "x", 1)
        else:
            src, to = slot_of(9 - step), along(me, -1)
        return send(
            chunk(src, number), chunk(slot_of(8 - step), number),
            halo_send.at[4 + step, number], halo_recv.at[4 + step, number], to,
        )

    def own_arrives(from_hi):
        src = half_ref.at[pl.ds(0, 128)]
        dst = kv_ref.at[0, pl.ds(from_hi * 128, 128)]
        send(src, dst, group_send.at[0], group_recv.at[from_hi], mate).wait_recv()

    for from_hi in range(2):
        own_arrives(from_hi)
        for number in range(2 * from_hi, 2 * from_hi + 2):
            forth(1, number).start()
            back(0, number).start()
    page = pool_ref.at[core * 32 + pair]
    send(half_ref.at[pl.ds(256, 16)], page, group_send.at[2], group_recv.at[2], mate).wait_recv()
    for copy in pool_copies(0):
        copy.start()

    def attend(first, count, masked, at):
        rows = count * PAIR
        head = at // 5
        query = query_ref[:, :, at * 128:at * 128 + 128].reshape(PAIR, 128)
        key = kv_ref[first:first + count, :, head * 128:head * 128 + 128].reshape(rows, 128)
        value = kv_ref[first:first + count, :, 256 + head * 128:384 + head * 128]
        score = lax.dot_general(
            query, key, (((1,), (1,)), ((), ())), preferred_element_type=jnp.float32
        )
        if masked:
            score = score + bias_ref[:, :rows]
        old = top_ref[at]
        new = jnp.maximum(old, jnp.max(score, axis=1, keepdims=True))
        factor = jnp.exp2((old - new) * SCALE)
        weight = jnp.exp2((score - jnp.concatenate([new] * (rows // 128), axis=1)) * SCALE)
        part = weight[:, :128]
        for lanes in range(128, rows, 128):
            part = part + weight[:, lanes:lanes + 128]
        top_ref[at] = new
        total_ref[at] = total_ref[at] * factor + part
        sum_ref[at] = sum_ref[at] * factor + jnp.dot(
            weight.astype(jnp.bfloat16), value.reshape(rows, 128),
            preferred_element_type=jnp.float32,
        )

    def give(at):
        first = pl.multiple_of(y_hi * HALF_WIDTH + at * 128, 128)
        return send(
            give_ref.at[:, pl.ds(at * 128, 128)], out_ref.at[:, pl.ds(first, 128)],
            give_send.at[at], give_recv.at[at], partner,
        )

    def finish(at):
        total = jnp.sum(total_ref[at], axis=1, keepdims=True)
        done = (sum_ref[at] / total).astype(jnp.bfloat16).reshape(2, 128, 128)
        for hi in range(2):
            @pl.when(y_hi == hi)
            def _():
                first = hi * HALF_WIDTH + at * 128
                out_ref[:, first:first + 128] = done[hi]
                give_ref[:, at * 128:at * 128 + 128] = done[1 - hi]
        give(at).start()

    def stage(step):
        bias_ref[:, :PAIR] = bias_of(step)
        bias_ref[:, PAIR:] = bias_of(9 - step)

    def prompt_in():
        pool_swap.wait_recv()

        def page_in(number, carry):
            first = pl.multiple_of(lax.rem(number, 16) * 16, 16)
            at = table_ref[0, number]
            kv_ref[9 + lax.div(number, 16), pl.ds(first, 16)] = pool_ref[
                lax.rem(at, 2) * 32 + lax.div(at, 2)
            ]
            return carry

        lax.fori_loop(0, 32, page_in, 0)

    def heads(number, parts):
        return range(10 * number // parts, 10 * (number + 1) // parts)

    for step in range(1, 4):
        for number in range(CHUNKS):
            forth(step, number).wait_recv()
            forth(step + 1, number).start()
            back(step - 1, number).wait_recv()
            back(step, number).start()
            if step == 2 and number == 0:
                for copy in pool_copies(0):
                    copy.wait_recv()
                for copy in pool_copies(1):
                    copy.start()
            if step == 3 and number == 1:
                for copy in pool_copies(1):
                    copy.wait_recv()
                pool_swap.start()
            if step == 1:
                if number == CHUNKS // 2:
                    query_out.wait_recv()
                    query_stay.wait()
                if number >= CHUNKS // 2:
                    for at in heads(number - CHUNKS // 2, CHUNKS - CHUNKS // 2):
                        attend(0, 1, True, at)
            else:
                for at in heads(number, CHUNKS):
                    attend(2 * step - 3, 2, True, at)
        stage(step)
    for at in range(10):
        attend(5, 2, True, at)
    prompt_in()
    for at in range(10):
        attend(9, 2, False, at)
    stage(4)
    for number in range(CHUNKS):
        forth(4, number).wait_recv()
        back(3, number).wait_recv()
    for at in range(10):
        attend(7, 2, True, at)
        finish(at)

    for at in range(10):
        give(at).wait()
    for copy in to_mate:
        copy.wait_send()
    rows_out.wait_send()
    query_out.wait_send()
    for part in range(PARTS):
        for phase in range(2):
            for copy in direct(part, phase):
                copy.wait_send()
        for step, way, half in ring_sends(part):
            ring(part, step, way, half).wait_send()
    for number in range(3):
        src, dst, to, stays = regroup(number, y_hi)

        @pl.when(jnp.logical_not(stays))
        def _():
            send(src, dst, group_send.at[number], group_recv.at[0], to).wait_send()

    for phase in range(2):
        for copy in pool_copies(phase):
            copy.wait_send()
    pool_swap.wait_send()
    for step in range(1, 5):
        for number in range(CHUNKS):
            forth(step, number).wait_send()
            back(step - 1, number).wait_send()


def body(hidden, queries, key_value_weight, pooled_hidden_states, group_page_table, resp_lengths):
    in_hbm = pl.BlockSpec(memory_space=pl.ANY)
    in_vmem = pl.BlockSpec(memory_space=pltpu.VMEM)
    in_smem = pl.BlockSpec(memory_space=pltpu.SMEM)
    dma = pltpu.SemaphoreType.DMA
    shards = pltpu.VMEM((2, 2, 4, 8, 2, 16, 128), jnp.bfloat16)
    sums = pltpu.VMEM((HALF_HEADS, PAIR, 128), jnp.float32)
    out = pl.pallas_call(
        kernel,
        name="attend",
        out_shape=jax.ShapeDtypeStruct((DEVICE_TOKENS, QUERY_HEADS * HEAD_SIZE), jnp.bfloat16),
        in_specs=[in_vmem, in_hbm, in_hbm, in_hbm, in_smem, in_smem],
        out_specs=in_vmem,
        scratch_shapes=[
            shards, shards, shards, shards, shards,
            pltpu.VMEM((2, 16, 128), jnp.bfloat16),
            pltpu.VMEM((ROWS, WIDTH), jnp.bfloat16),
            pltpu.VMEM((640, 640), jnp.bfloat16),
            pltpu.VMEM((ROWS, 4096), jnp.bfloat16),
            pltpu.VMEM((ROWS, 1024), jnp.bfloat16),
            pltpu.VMEM((4096, 128), jnp.float32),
            pltpu.VMEM((ROWS, 512), jnp.bfloat16),
            pltpu.VMEM((11, PAIR, 512), jnp.bfloat16),
            pltpu.VMEM((64, PAGE_TOKENS, 512), jnp.bfloat16),
            pltpu.VMEM((2, DEVICE_TOKENS, HALF_WIDTH), jnp.bfloat16),
            pltpu.VMEM((DEVICE_TOKENS, HALF_WIDTH), jnp.bfloat16),
            pltpu.VMEM((PAIR, 2 * PAIR), jnp.float32),
            pltpu.VMEM((PAIR, PAIR), jnp.int32),
            sums, sums, sums,
            dma((PARTS, 26)), dma((PARTS, 26)), dma((6,)), dma((6,)), dma((8,)),
            dma((3,)), dma((3,)), dma, dma,
            dma((8, CHUNKS)), dma((8, CHUNKS)), dma((11,)), dma((11,)),
            dma((HALF_HEADS,)), dma((HALF_HEADS,)),
        ],
        compiler_params=pltpu.CompilerParams(
            collective_id=0, has_side_effects=True, vmem_limit_bytes=56 * 1024 * 1024
        ),
    )(
        key_value_weight, hidden[0], pooled_hidden_states[0], queries[0],
        group_page_table, resp_lengths,
    )
    return out[None]


def solution(mesh):
    in_specs = (
        P("group", "ctx", None),
        P("group", "ctx", None),
        P(("group", "ctx"), None),
        P("ctx", None, None),
        P("group", None),
        P("group", None),
    )
    out_specs = P("group", "ctx", None)
    return jax.shard_map(body, mesh=mesh, in_specs=in_specs, out_specs=out_specs, check_vma=False)
```
